512 devices in a mesh: mem: 128 (over x, z_hi, y, core), tile: 4 (over z_lo).
Axes of the slice: x: 4, y: 8, z: 8 (z_hi: 2, z_lo: 4; z = z_hi * 4 + z_lo), core: 2. Of those that a mesh axis runs over, the one named last changes fastest.
Arguments:
- state: float32 [4, 8, 256, 16, 512], P(None, None, 'mem', 'tile'), may hold values from -5 to 5, as said below
- branch: int32 [16, 512], replicated, may hold values from 0 to 2
- obs_site: int32 [4, 1024], P('tile'), may hold values from 0 to 65535
- obs_value: float32 [4, 1024], P('tile'), may hold values from -6 to 6
- patch_index: int32 [4, 2048, 128], P('tile'), may hold values from 0 to 1023
- patch_weight: float32 [4, 2048, 128], P('tile', 'mem'), may hold values from 0.1 to 4
Outputs:
- analysis: float32 [4, 8, 256, 16, 512], P(None, None, 'mem', 'tile')
The draws below stay inside these ranges and needn't reach their ends.
Inputs may be any that keep to these rules, and one draw needn't show every extreme that they name: `state`: variable 3 (turbulent kinetic energy) is positive.
All inputs are finite; a program needn't handle non-finite values.
Results may differ from the reference program's by a relative error of at most 0.0003.
Values sent between devices are 32-bit elements; how exact they have to be, the bound alone decides.
A program may use at most 128 MiB of HBM per device.

```python
import math
import jax
import jax.numpy as jnp
from jax import lax

UNKNOWNS_TOTAL = 4
MEM_DEV = 2
STRATUM_TOTAL = 8
COL_A = 16
OBS_TILE = 1024
P_SIZE = 128
NS_ITERS = 3
REALIZATIONS = 256
NORTHWARD_POINTS = 512
PATCH_WIDTH = 2048
EASTWARD_POINTS = 16
N_MEM = 128
N_TILE = 4


def draw_state(key, part):
    key = jax.random.fold_in(key, 11)
    wind_key, energy_key = jax.random.split(key)
    wind_shape = (UNKNOWNS_TOTAL - 1, STRATUM_TOTAL, REALIZATIONS, EASTWARD_POINTS, NORTHWARD_POINTS)
    winds = jnp.clip(jax.random.normal(wind_key, wind_shape, jnp.float32), -5.0, 5.0)
    energy = jnp.exp(jax.random.uniform(energy_key, (1, STRATUM_TOTAL, REALIZATIONS, EASTWARD_POINTS, NORTHWARD_POINTS), jnp.float32, math.log(0.05), math.log(2.0)))
    return jnp.concatenate([winds, energy], axis=0)


def touch_ends(array, own_key, smallest, top_value):
    index_at = [jax.random.randint(jax.random.fold_in(own_key, axis), (), 0, length) for axis, length in enumerate(array.shape)]
    longest = array.shape.index(max(array.shape))
    next_to = index_at[:longest] + [(index_at[longest] + 1) % array.shape[longest]] + index_at[longest + 1:]
    return array.at[tuple(index_at)].set(smallest).at[tuple(next_to)].set(top_value)


def steps_of(stream_key, dims, pieces, least, high):
    def one(position, parts):
        draws = jax.random.uniform(jax.random.fold_in(jax.random.fold_in(stream_key, 6), position), (parts,), jnp.float32, least / len(pieces), high / len(pieces))
        return jnp.repeat(jnp.exp(draws), dims[position] // parts).reshape((-1,) + (1,) * (len(dims) - position - 1))

    factor_of = one(*pieces[0])
    for cut in pieces[1:]:
        factor_of = factor_of * one(*cut)
    return factor_of


def gaussian(key, dims, scale, reach, shards=(), held_as=jnp.bfloat16):
    drawn = jax.random.normal(key, dims, jnp.float32) * scale
    if len(shards) > 0:
        drawn = steps_of(key, dims, shards, -0.22, 0.18) * drawn
    return jnp.clip(drawn, min=-reach, max=reach).astype(held_as)


def setup_inputs(seed: int = 0) -> dict:
    seeds = jax.random.split(jax.random.key(seed), 7)
    return {
        "state": draw_state(jax.random.fold_in(seeds[6], 71), 0),
        "branch": touch_ends(jax.random.randint(seeds[1], (EASTWARD_POINTS, NORTHWARD_POINTS), 0, 3), jax.random.fold_in(seeds[1], 1), 0, 2).astype(jnp.int32),
        "obs_site": touch_ends(jax.random.randint(seeds[2], (N_TILE, OBS_TILE), 0, UNKNOWNS_TOTAL * STRATUM_TOTAL * PATCH_WIDTH), jax.random.fold_in(seeds[2], 1), 0, (UNKNOWNS_TOTAL * STRATUM_TOTAL * PATCH_WIDTH) - 1).astype(jnp.int32),
        "obs_value": gaussian(seeds[3], (N_TILE, OBS_TILE), 1.0, 6.0, ((0, 4),), jnp.float32),
        "patch_index": touch_ends(jax.random.randint(seeds[4], (N_TILE, PATCH_WIDTH, P_SIZE), 0, OBS_TILE), jax.random.fold_in(seeds[4], 1), 0, OBS_TILE - 1).astype(jnp.int32),
        "patch_weight": jnp.clip(jnp.exp(math.log(4.0) - 3.6888794 * jax.random.uniform(seeds[5], (N_TILE, PATCH_WIDTH, P_SIZE), jnp.float32) ** steps_of(seeds[5], (N_TILE, PATCH_WIDTH, P_SIZE), ((0, 4), (1, 128)), -0.2, 0.2)), 0.1, 4.0),
    }


def coefficients(branch):
    stable_m = jnp.where(branch == 0, 0.25, jnp.where(branch == 1, 0.6, 1.2)).astype(jnp.float32)
    stable_h = jnp.where(branch == 0, 0.15, jnp.where(branch == 1, 0.7, 1.6)).astype(jnp.float32)
    return (stable_m, stable_h)

def diffuse(padded):
    centre = padded[:, :, :, 1:-1]
    laplace = padded[:, :, :, 2:] + padded[:, :, :, :-2] + jnp.roll(centre, 1, -1) + jnp.roll(centre, -1, -1) - 4.0 * centre
    return centre + 0.2 * laplace

def thomas(below, above, extra, rhs):
    levels = rhs.shape[0]
    diagonal_terms = 1.0 + below + above + extra
    ratios = []
    values = []
    for height in range(levels):
        if height == 0:
            pivots = diagonal_terms[0]
            solved = rhs[0] / pivots
        else:
            pivots = diagonal_terms[height] - below[height] * ratios[-1]
            solved = (rhs[height] + below[height] * values[-1]) / pivots
        ratios.append(above[height] / pivots)
        values.append(solved)
    result = [values[-1]]
    for height in range(levels - 2, -1, -1):
        result.append(values[height] + ratios[height] * result[-1])
    return jnp.stack(result[::-1])

def column_step(model_quantities, stable_m, stable_h):
    wind_u, wind_v, theta_field, energy = (model_quantities[0], model_quantities[1], model_quantities[2], model_quantities[3])
    face_energy = 0.5 * (energy[:-1] + energy[1:])
    velocity_scale = 0.6 * jnp.sqrt(face_energy)
    mix_momentum = velocity_scale * stable_m
    mix_heat = velocity_scale * stable_h
    shear_sq = (wind_u[1:] - wind_u[:-1]) ** 2 + (wind_v[1:] - wind_v[:-1]) ** 2
    face_production = mix_momentum * shear_sq
    zeros_row = jnp.zeros_like(face_production[:1])
    production = 0.5 * (jnp.concatenate([zeros_row, face_production]) + jnp.concatenate([face_production, zeros_row]))
    mom_below = jnp.concatenate([zeros_row, mix_momentum])
    mom_above = jnp.concatenate([mix_momentum, zeros_row])
    heat_below = jnp.concatenate([zeros_row, mix_heat])
    heat_above = jnp.concatenate([mix_heat, zeros_row])
    dissipation = 0.3 * jnp.sqrt(energy)
    new_u = thomas(mom_below, mom_above, 0.0, wind_u)
    new_v = thomas(mom_below, mom_above, 0.0, wind_v)
    new_theta = thomas(heat_below, heat_above, 0.0, theta_field)
    new_energy = thomas(mom_below, mom_above, dissipation, energy + production)
    return jnp.stack([new_u, new_v, new_theta, new_energy])

def analyze(columns, obs_ens, obs_vals, weights):
    highest = lax.Precision.HIGHEST
    members = obs_ens.shape[2]
    obs_mean = lax.optimization_barrier(jnp.mean(obs_ens, axis=2))
    obs_pert = obs_ens - obs_mean[:, :, None]
    weighted = obs_pert * weights[:, :, None]
    identity = jnp.eye(members, dtype=jnp.float32)
    gram_matrix = identity + jnp.einsum('cpk,cpj->ckj', weighted, obs_pert, precision=highest) / (members - 1.0)
    frobenius = jnp.sqrt(lax.optimization_barrier(jnp.sum(gram_matrix * gram_matrix, axis=(1, 2))))
    iterate = gram_matrix / frobenius[:, None, None]
    factor = 0.5 * (3.0 * identity - iterate)
    iterate = jnp.matmul(iterate, factor, precision=highest)
    inverse = factor
    for number in range(1, NS_ITERS):
        factor = 0.5 * (3.0 * identity - jnp.matmul(inverse, iterate, precision=highest))
        inverse = jnp.matmul(factor, inverse, precision=highest)
        if number + 1 < NS_ITERS:
            iterate = jnp.matmul(iterate, factor, precision=highest)
    transform = inverse / jnp.sqrt(frobenius)[:, None, None]
    forcing = jnp.einsum('cpk,cp->ck', weighted, obs_vals - obs_mean, precision=highest)
    inner_step = jnp.einsum('ckj,cj->ck', transform, forcing, precision=highest)
    mean_weight = jnp.einsum('ckj,cj->ck', transform, inner_step, precision=highest) / (members - 1.0)
    state_mean = lax.optimization_barrier(jnp.mean(columns, axis=1))
    state_pert = columns - state_mean[:, None, :]
    spread = jnp.einsum('vjc,cjk->vkc', state_pert, transform, precision=highest)
    centre = state_mean + jnp.einsum('vjc,cj->vc', state_pert, mean_weight, precision=highest)
    return centre[:, None, :] + spread

def reference(state, branch, obs_site, obs_value, patch_index, patch_weight):
    stable_m, stable_h = coefficients(branch)
    profile_partitions = state.reshape(UNKNOWNS_TOTAL, STRATUM_TOTAL, REALIZATIONS // MEM_DEV, MEM_DEV, EASTWARD_POINTS, NORTHWARD_POINTS).transpose(2, 0, 1, 3, 4, 5)

    def partition_prediction(model_quantities):
        for timestep in range(2):
            padded = jnp.concatenate([model_quantities[:, :, :, -1:], model_quantities, model_quantities[:, :, :, :1]], axis=3)
            model_quantities = column_step(diffuse(padded), stable_m, stable_h)
        return model_quantities
    collective_prediction = lax.map(partition_prediction, profile_partitions).transpose(1, 2, 0, 3, 4, 5).reshape(UNKNOWNS_TOTAL, STRATUM_TOTAL, REALIZATIONS, EASTWARD_POINTS, NORTHWARD_POINTS)
    domain_partitions = collective_prediction.reshape(UNKNOWNS_TOTAL * STRATUM_TOTAL, REALIZATIONS, N_TILE, PATCH_WIDTH).transpose(2, 0, 1, 3)
    site_rows = obs_site // PATCH_WIDTH
    site_cols = obs_site % PATCH_WIDTH
    obs_all = jax.vmap(lambda tile_state, rows_of, cols_of: tile_state[rows_of, :, cols_of])(domain_partitions, site_rows, site_cols)

    def analyse_block(index):
        tile_index = index // N_MEM
        member_index = index % N_MEM
        tile_state = lax.dynamic_index_in_dim(domain_partitions, tile_index, 0, keepdims=False)
        columns = lax.dynamic_slice_in_dim(tile_state, member_index * COL_A, COL_A, 2)
        tile_patch = lax.dynamic_index_in_dim(patch_index, tile_index, 0, keepdims=False)
        own_patch = lax.dynamic_slice_in_dim(tile_patch, member_index * COL_A, COL_A, 0)
        tile_obs = lax.dynamic_index_in_dim(obs_all, tile_index, 0, keepdims=False)
        tile_values = lax.dynamic_index_in_dim(obs_value, tile_index, 0, keepdims=False)
        tile_weight = lax.dynamic_index_in_dim(patch_weight, tile_index, 0, keepdims=False)
        weights = lax.dynamic_slice_in_dim(tile_weight, member_index * COL_A, COL_A, 0)
        return analyze(columns, tile_obs[own_patch], tile_values[own_patch], weights)
    result = lax.map(analyse_block, jnp.arange(N_TILE * N_MEM, dtype=jnp.int32))
    result = result.reshape(N_TILE, N_MEM, UNKNOWNS_TOTAL * STRATUM_TOTAL, REALIZATIONS, COL_A).transpose(2, 3, 0, 1, 4)
    return result.reshape(UNKNOWNS_TOTAL, STRATUM_TOTAL, REALIZATIONS, EASTWARD_POINTS, NORTHWARD_POINTS)
```

```python
import jax
import jax.numpy as jnp
from jax import lax
from jax.experimental import pallas as pl
from jax.experimental.pallas import tpu as pltpu
from jax.sharding import PartitionSpec as P

MESH = pl.DeviceIdType.MESH
F32 = jnp.float32
BF16 = jnp.bfloat16
VMEM = pl.BlockSpec(memory_space=pltpu.VMEM)
ANY = pl.BlockSpec(memory_space=pl.ANY)
LEVELS, ROWS, WIDTH, LANES = 8, 32, 512, 128
MEM, COLS, MEMBERS, PATCH, OBS = 128, 16, 256, 128, 1024


def rem(a, b):
    return lax.rem(a, jnp.int32(b))


def div(a, b):
    return lax.div(a, jnp.int32(b))


def slot_of(device):
    core, y = rem(device, 2), rem(div(device, 2), 8)
    z, x = rem(div(device, 16), 2), div(device, 32)
    return core * 64 + x * 16 + y * 2 + z


def device_at(core, x, y, z):
    return x * 32 + z * 16 + y * 2 + core


def wait_rows(ref, sem, rows):
    part = ref.at[pl.ds(0, rows)]
    pltpu.make_async_copy(part, part, sem).wait()


def send(src, dst, send_sem, recv_sem, mem, tile):
    pltpu.make_async_remote_copy(
        src_ref=src, dst_ref=dst, send_sem=send_sem, recv_sem=recv_sem,
        device_id=(mem, tile), device_id_type=MESH,
    ).start()


def block_transpose(blocks):
    group = lax.broadcasted_iota(jnp.int32, (8, LANES), 1) // 16
    blocks = list(blocks)
    for bit in (1, 2, 4):
        upper = (group // bit) % 2 == 1
        for low in range(8):
            if low & bit:
                continue
            a, b = blocks[low], blocks[low + bit]
            blocks[low] = jnp.where(upper, pltpu.roll(b, 16 * bit, 1), a)
            blocks[low + bit] = jnp.where(upper, b, pltpu.roll(a, LANES - 16 * bit, 1))
    return blocks


def column_step(u, v, theta, energy, stab_m, stab_h):
    n = LEVELS
    km, kh, prod = [], [], []
    for k in range(n - 1):
        scale = 0.6 * jnp.sqrt(0.5 * (energy[k] + energy[k + 1]))
        km.append(scale * stab_m)
        kh.append(scale * stab_h)
        du, dv = u[k + 1] - u[k], v[k + 1] - v[k]
        prod.append(km[k] * (du * du + dv * dv))

    def solve(coef, extra, rhs):
        count = len(rhs)
        ratios, values = [], [[] for _ in range(count)]
        for k in range(n):
            pivot = 1.0 + extra[k] if extra is not None else 1.0
            if k > 0:
                pivot = pivot + coef[k - 1]
            if k < n - 1:
                pivot = pivot + coef[k]
            if k > 0:
                pivot = pivot - coef[k - 1] * ratios[-1]
            inverse = 1.0 / pivot
            for i in range(count):
                top = rhs[i][k]
                if k > 0:
                    top = top + coef[k - 1] * values[i][-1]
                values[i].append(top * inverse)
            if k < n - 1:
                ratios.append(coef[k] * inverse)
        out = []
        for i in range(count):
            result = [values[i][n - 1]]
            for k in range(n - 2, -1, -1):
                result.append(values[i][k] + ratios[k] * result[-1])
            out.append(result[::-1])
        return out

    source = []
    for k in range(n):
        if k == 0:
            total = prod[0]
        elif k == n - 1:
            total = prod[n - 2]
        else:
            total = prod[k - 1] + prod[k]
        source.append(energy[k] + 0.5 * total)
    sink = [0.3 * jnp.sqrt(energy[k]) for k in range(n)]
    new_u, new_v = solve(km, None, [u, v])
    (new_theta,) = solve(kh, None, [theta])
    (new_energy,) = solve(km, sink, [source])
    return new_u, new_v, new_theta, new_energy


def stabilities(branch):
    m = jnp.where(branch == 0, 0.25, jnp.where(branch == 1, 0.6, 1.2)).astype(F32)
    h = jnp.where(branch == 0, 0.15, jnp.where(branch == 1, 0.7, 1.6)).astype(F32)
    return m, h


def mix_columns(src, dst, stab_ref):
    def body(lt, carry):
        base = pl.multiple_of(lt * 256, 256)
        field = [[src[pl.ds(base + (var * 8 + k) * 8, 8), :] for k in range(LEVELS)] for var in range(4)]
        sbase = pl.multiple_of(lt * 16, 16)
        stab_m, stab_h = stab_ref[pl.ds(sbase, 8), :], stab_ref[pl.ds(sbase + 8, 8), :]
        new = column_step(*field, stab_m, stab_h)
        for var in range(4):
            for k in range(LEVELS):
                dst[pl.ds(base + (var * 8 + k) * 8, 8), :] = new[var][k]
        return carry
    lax.fori_loop(0, 4, body, 0)


def rows_of(ref, row):
    return jnp.broadcast_to(ref[pl.ds(row, 1), :], (8, WIDTH))


def laplace_step(centre, up, down):
    total = up + down + pltpu.roll(centre, 1, 1) + pltpu.roll(centre, WIDTH - 1, 1) - 4.0 * centre
    return centre + 0.2 * total


def put_tiles(dst, row, value):
    for lt in range(4):
        dst[pl.ds(pl.multiple_of(lt * 256 + row * 8, 8), 8), :] = value[:, lt * LANES:(lt + 1) * LANES]


def get_tiles(src, row):
    return jnp.concatenate(
        [src[pl.ds(pl.multiple_of(lt * 256 + row * 8, 8), 8), :] for lt in range(4)], axis=1)


def forecast_body(state, branch, stab, stab_edge, to_next, to_prev, from_prev, from_next, mixed, edge, halo_send, halo_recv, me, tile):
    sub = lax.broadcasted_iota(jnp.int32, (8, WIDTH), 0)
    next_tile, prev_tile = rem(tile + 1, 4), rem(tile + 3, 4)

    def pack(row, carry):
        for q, (n_sub, p_sub) in enumerate(((3, 0), (7, 4), (2, 1), (6, 5))):
            to_next[pl.ds(row * 4 + q, 1), :] = state[row, pl.ds(n_sub, 1), :]
            to_prev[pl.ds(row * 4 + q, 1), :] = state[row, pl.ds(p_sub, 1), :]
        return carry
    lax.fori_loop(0, ROWS, pack, 0)
    send(to_next, from_prev, halo_send.at[0], halo_recv.at[0], me, next_tile)
    send(to_prev, from_next, halo_send.at[1], halo_recv.at[1], me, prev_tile)

    own = [rows_of(branch, tile * 4 + x) for x in range(4)]
    before, after = rows_of(branch, rem(tile * 4 + 15, 16)), rows_of(branch, rem(tile * 4 + 4, 16))
    x_of = sub % 4
    own_rows = jnp.where(x_of == 0, own[0], jnp.where(x_of == 1, own[1], jnp.where(x_of == 2, own[2], own[3])))
    edge_rows = jnp.where(x_of < 2, before, after)
    for ref, rows in ((stab, own_rows), (stab_edge, edge_rows)):
        m, h = stabilities(rows)
        for lt in range(4):
            ref[pl.ds(lt * 16, 8), :] = m[:, lt * LANES:(lt + 1) * LANES]
            ref[pl.ds(lt * 16 + 8, 8), :] = h[:, lt * LANES:(lt + 1) * LANES]

    wait_rows(to_next, halo_send.at[0], 128)
    wait_rows(to_prev, halo_send.at[1], 128)
    wait_rows(from_prev, halo_recv.at[0], 128)
    wait_rows(from_next, halo_recv.at[1], 128)

    def pick(a, b, c, d):
        return jnp.where(x_of == 0, a, jnp.where(x_of == 1, b, jnp.where(x_of == 2, c, d)))

    def first(row, carry):
        centre = state[row]
        left = [rows_of(from_prev, row * 4 + q) for q in range(4)]
        right = [rows_of(from_next, row * 4 + q) for q in range(4)]
        up = jnp.where(x_of == 0, jnp.where(sub < 4, left[0], left[1]), pltpu.roll(centre, 1, 0))
        down = jnp.where(x_of == 3, jnp.where(sub < 4, right[0], right[1]), pltpu.roll(centre, 7, 0))
        put_tiles(mixed, row, laplace_step(centre, up, down))
        inner = [jnp.broadcast_to(state[row, pl.ds(s, 1), :], (8, WIDTH)) for s in (0, 4, 3, 7)]
        edge_centre = pick(left[0], left[1], right[0], right[1])
        outer = pick(left[2], left[3], right[2], right[3])
        put_tiles(edge, row, laplace_step(edge_centre, outer, pick(*inner)))
        return carry
    lax.fori_loop(0, ROWS, first, 0)
    mix_columns(mixed, mixed, stab)
    mix_columns(edge, edge, stab_edge)

    def second(row, carry):
        centre = get_tiles(mixed, row)
        sides = get_tiles(edge, row)
        side = [jnp.broadcast_to(sides[q:q + 1, :], (8, WIDTH)) for q in range(4)]
        up = jnp.where(x_of == 0, jnp.where(sub < 4, side[0], side[1]), pltpu.roll(centre, 1, 0))
        down = jnp.where(x_of == 3, jnp.where(sub < 4, side[2], side[3]), pltpu.roll(centre, 7, 0))
        put_tiles(mixed, row, laplace_step(centre, up, down))
        return carry
    lax.fori_loop(0, ROWS, second, 0)
    mix_columns(mixed, mixed, stab)


def observe(mixed, site, obs):
    sub = lax.broadcasted_iota(jnp.int32, (8, LANES), 0)
    sites = site[...]
    lane, x = sites % 128, (sites // 512) % 4
    key = (sites // 2048) * 4 + (sites // 128) % 4

    def spread(a, b):
        return jnp.broadcast_to(a[b:b + 1, :], (8, LANES))
    lanes = [spread(lane, b) for b in range(8)]
    keys = [spread(key, b) for b in range(8)]

    def body(row, accs):
        accs = list(accs)
        for lt in range(4):
            tile = mixed[pl.ds(pl.multiple_of(lt * 256 + row * 8, 8), 8), :]
            for b in range(8):
                found = jnp.take_along_axis(tile, lanes[b], axis=1, mode="promise_in_bounds")
                accs[b] = jnp.where(keys[b] == row * 4 + lt, found, accs[b])
        return tuple(accs)
    accs = lax.fori_loop(0, ROWS, body, tuple(jnp.zeros((8, LANES), F32) for _ in range(8)))
    for b in range(8):
        only = jnp.where(sub % 4 == spread(x, b), accs[b], 0.0)
        only = only + pltpu.roll(only, 7, 0)
        only = only + pltpu.roll(only, 6, 0)
        obs[pl.ds(b, 1), :] = only[0:1, :]
        obs[pl.ds(8 + b, 1), :] = only[4:5, :]


def cut_columns(mixed, tiles):
    def body(n, carry):
        x, lt = div(n, 4), rem(n, 4)
        blocks = [mixed[pl.ds(lt * 256 + var * 64 + m * 4 + x, 8, stride=8), :] for m in range(2) for var in range(4)]
        for g, block in enumerate(block_transpose(blocks)):
            tiles[pl.ds(pl.multiple_of((x * 32 + lt * 8 + g) * 8, 8), 8), :] = block
        return carry
    lax.fori_loop(0, 16, body, 0)


def gather_obs(table, sems, me, tile):
    core, y, z, x = rem(me, 2), rem(div(me, 2), 8), rem(div(me, 16), 2), div(me, 32)
    mine = table.at[pl.ds(pl.multiple_of(slot_of(me) * 16, 16), 16)]
    send(mine, mine, sems.at[0], sems.at[1], device_at(core, x, y, 1 - z), tile)
    yield
    wait_rows(table, sems.at[0], 16)
    wait_rows(table, sems.at[1], 16)
    pair = table.at[pl.ds(pl.multiple_of((core * 64 + x * 16 + y * 2) * 16, 32), 32)]
    for i in range(1, 8):
        send(pair, pair, sems.at[2], sems.at[3], device_at(core, x, rem(y + i, 8), z), tile)
    yield
    wait_rows(table, sems.at[2], 32 * 7)
    wait_rows(table, sems.at[3], 32 * 7)
    plane = table.at[pl.ds(pl.multiple_of((core * 64 + x * 16) * 16, 256), 256)]
    for i in range(1, 4):
        send(plane, plane, sems.at[4], sems.at[5], device_at(core, rem(x + i, 4), y, z), tile)
    yield
    wait_rows(table, sems.at[4], 256 * 3)
    wait_rows(table, sems.at[5], 256 * 3)
    half = table.at[pl.ds(pl.multiple_of(core * 1024, 1024), 1024)]
    send(half, half, sems.at[6], sems.at[7], device_at(1 - core, x, y, z), tile)
    yield
    wait_rows(table, sems.at[6], 1024)
    wait_rows(table, sems.at[7], 1024)


def greet(me, tile, with_tiles):
    barrier = pltpu.get_barrier_semaphore()
    count = MEM - 1
    if with_tiles:
        for step in (1, 3):
            pl.semaphore_signal(barrier, inc=1, device_id=(me, rem(tile + step, 4)), device_id_type=MESH)
        count += 2

    def body(i, carry):
        pl.semaphore_signal(barrier, inc=1, device_id=(rem(me + i, MEM), tile), device_id_type=MESH)
        return carry
    lax.fori_loop(1, MEM, body, 0)
    pl.semaphore_wait(barrier, count)


def forecast_kernel(state, branch, site, columns, table,
                    stab, stab_edge, to_next, to_prev, from_prev, from_next, mixed, edge, tiles, obs,
                    halo_send, halo_recv, gather_sems, out_sem, in_sem, own_sem):
    me, tile = lax.axis_index("mem"), lax.axis_index("tile")
    greet(me, tile, True)
    forecast_body(state, branch, stab, stab_edge, to_next, to_prev, from_prev, from_next, mixed, edge, halo_send, halo_recv, me, tile)
    observe(mixed, site, obs)
    slot = slot_of(me)
    table[pl.ds(pl.multiple_of(slot * 16, 16), 16), :] = obs[...]
    gather = gather_obs(table, gather_sems, me, tile)
    next(gather)
    cut_columns(mixed, tiles)
    next(gather)
    next(gather)
    here = pl.ds(pl.multiple_of(slot * 8, 8), 8)

    def body(i, carry):
        to = rem(me + i, MEM)
        send(tiles.at[pl.ds(pl.multiple_of(to * 8, 8), 8)], columns.at[here], out_sem, in_sem, to, tile)
        return carry
    lax.fori_loop(1, MEM, body, 0)
    columns[here, :] = tiles[pl.ds(pl.multiple_of(me * 8, 8), 8), :]
    next(gather)
    for _ in gather:
        pass
    wait_rows(tiles, out_sem, 8 * (MEM - 1))
    wait_rows(columns, in_sem, 8 * (MEM - 1))


def split(a):
    high = a.astype(BF16)
    return high, (a - high.astype(F32)).astype(BF16)


def dot(a, b):
    return jnp.dot(a, b, preferred_element_type=F32)


def dot_t(a, b):
    return lax.dot_general(a, b, (((1,), (1,)), ((), ())), preferred_element_type=F32)


def dot3(a, pair):
    high, low = split(a)
    return dot(high, pair[0]) + (dot(low, pair[0]) + dot(high, pair[1]))


def prepare(columns, table, value, index, weight, fields, lookup, turned, gap):
    total = table[pl.ds(0, 16), :]
    total = lax.fori_loop(1, MEM, lambda s, t: t + table[pl.ds(pl.multiple_of(s * 16, 16), 16), :], total)
    mean = (total[:8] + total[8:]) * (1.0 / MEMBERS)
    diff = value[...] - mean
    for b in range(8):
        for m in range(2):
            block = table[pl.ds(m * 8 + b, MEM, stride=16), :] - mean[b:b + 1, :]
            high, low = split(jnp.transpose(block))
            lookup[pl.ds(b * 128, 128), pl.ds(m * 128, 128)] = high
            lookup[pl.ds(b * 128, 128), pl.ds(256 + m * 128, 128)] = low
    for level in range(LEVELS):
        fields[pl.ds(level * 128, 128), :] = jnp.transpose(columns[pl.ds(level, MEM, stride=8), :])
    indices = index[...]
    both = jnp.concatenate([indices.astype(F32), weight[...], jnp.zeros((96, LANES), F32)], axis=0)
    turned[...] = jnp.transpose(both)
    for part in range(2):
        own = indices[part * 8:part * 8 + 8]
        found = jnp.zeros((8, LANES), F32)
        for b in range(8):
            row = jnp.broadcast_to(diff[b:b + 1, :], (8, LANES))
            taken = jnp.take_along_axis(row, own % 128, axis=1, mode="promise_in_bounds")
            found = jnp.where(own // 128 == b, taken, found)
        gap[pl.ds(part * 8, 8), :] = found


def one_column(c, index_col, weight_col, weight, fields, lookup, gap, analysed):
    eye = (lax.broadcasted_iota(jnp.int32, (PATCH, PATCH), 0) == lax.broadcasted_iota(jnp.int32, (PATCH, PATCH), 1)).astype(F32)
    places = lax.broadcasted_iota(jnp.int32, (PATCH, OBS), 1)
    chosen = (places == index_col.astype(jnp.int32)).astype(F32).astype(BF16)
    picked = dot(chosen, lookup[...])
    high, low = picked[:, :MEMBERS].astype(BF16), picked[:, MEMBERS:].astype(BF16)
    rows = [(m * 4 + var) * 16 + c for m in range(2) for var in range(4)]
    parts = [fields[pl.ds(r, 8, stride=128), :] for r in rows]
    x = jnp.concatenate([jnp.concatenate(parts[:4], axis=0), jnp.concatenate(parts[4:], axis=0)], axis=1)
    mean = jnp.sum(x, axis=1, keepdims=True) * (1.0 / MEMBERS)
    pert = x - mean
    pert_high, pert_low = split(pert)
    top, bottom = jnp.concatenate([high, pert_high], axis=0), jnp.concatenate([low, pert_low], axis=0)
    products = dot_t(top, high) + (dot_t(top, low) + dot_t(bottom, high))
    w = weight[pl.ds(c, 1), :]
    cov = products[:PATCH]
    cov_w = cov * (w * (1.0 / (MEMBERS - 1.0)))
    cross_w = products[PATCH:] * (w * (1.0 / (MEMBERS - 1.0)))
    trace = jnp.sum(cov_w * eye, keepdims=True)
    square = jnp.sum(cov_w * cov * (weight_col * (1.0 / (MEMBERS - 1.0))), keepdims=True)
    norm = jnp.sqrt(MEMBERS + 2.0 * trace + square)
    inv = 1.0 / norm
    step = (eye + cov_w) * inv
    step_pair = split(step)
    cross = jnp.concatenate([cross_w * inv, jnp.zeros((8, PATCH), F32)], axis=0)
    first_row = lax.broadcasted_iota(jnp.int32, (8, PATCH), 0) == 0
    force = jnp.where(first_row, w * gap[pl.ds(c, 1), :], 0.0)
    square_step = dot3(step, step_pair)
    inner = 2.25 * eye - 1.5 * step + 0.25 * square_step
    turn_pair = split(dot3(inner, step_pair))
    rate = 1.5 - 0.5 * inv
    start = dot3(jnp.concatenate([cross[:ROWS], force], axis=0), step_pair)
    zero8 = jnp.zeros((8, PATCH), F32)
    v = 1.5 * cross[:ROWS] - 0.5 * (start[:ROWS] + inv * cross[:ROWS])
    a_v = inv * rate
    v = 1.5 * v - 0.5 * (dot3(v, step_pair) + a_v * cross[:ROWS])
    t1 = a_v * rate
    v = jnp.concatenate([v, zero8], axis=0)
    u = jnp.concatenate([-0.5 * cross[:ROWS], 1.5 * force - 0.5 * start[ROWS:]], axis=0)
    a = rate

    def times_t1(a, u):
        return a * t1, dot3(u, turn_pair) + a * v

    def times_f1(a, u):
        a2, u2 = times_t1(a, u)
        return 1.5 * a - 0.5 * a2, 1.5 * u - 0.5 * u2
    a, u = times_f1(a, u)
    a2, u2 = times_f1(*times_f1(*times_t1(a, u)))
    a, u = 1.5 * a - 0.5 * a2, 1.5 * u - 0.5 * u2
    spread = dot3(u, (high, low))
    scale = 1.0 / jnp.sqrt(norm)
    moved = (a * pert + spread[:ROWS]) * scale
    nudge = spread[ROWS:ROWS + 1] * scale
    centre = mean + jnp.sum(moved * nudge, axis=1, keepdims=True) * (1.0 / (MEMBERS - 1.0))
    out = moved + centre
    for m in range(2):
        for var in range(4):
            analysed[pl.ds((m * 4 + var) * 16 + c, 8, stride=128), :] = out[var * 8:var * 8 + 8, m * 128:m * 128 + 128]


UNROLL = 2


def analysis_kernel(columns, table, value, index_all, weight, outgoing, index, fields, lookup, turned, gap, analysed, sem):
    me = lax.axis_index("mem")
    copy = pltpu.make_async_copy(index_all.at[0, pl.ds(pl.multiple_of(me * COLS, COLS), COLS)], index, sem)
    copy.start()
    copy.wait()
    prepare(columns, table, value, index, weight, fields, lookup, turned, gap)

    def body(n, carry):
        here = pltpu.roll(turned[...], LANES - n * UNROLL, 1)
        for i in range(UNROLL):
            one_column(n * UNROLL + i, here[:, i:i + 1], here[:, COLS + i:COLS + i + 1], weight, fields, lookup, gap, analysed)
        return carry
    lax.fori_loop(0, COLS // UNROLL, body, 0)
    for level in range(LEVELS):
        outgoing[pl.ds(level, MEM, stride=8), :] = jnp.transpose(analysed[pl.ds(level * 128, 128), :])


def return_kernel(outgoing, result, landed, out_sem, in_sem):
    me, tile = lax.axis_index("mem"), lax.axis_index("tile")
    greet(me, tile, False)
    here = pl.ds(pl.multiple_of(me * 8, 8), 8)

    def body(i, carry):
        to = rem(me + i, MEM)
        send(outgoing.at[pl.ds(pl.multiple_of(slot_of(to) * 8, 8), 8)], landed.at[here], out_sem, in_sem, to, tile)
        return carry
    lax.fori_loop(1, MEM, body, 0)
    landed[here, :] = outgoing[pl.ds(pl.multiple_of(slot_of(me) * 8, 8), 8), :]
    wait_rows(outgoing, out_sem, 8 * (MEM - 1))
    wait_rows(landed, in_sem, 8 * (MEM - 1))
    place(landed, result)


def place(landed, result):
    def body(n, carry):
        x, lt = div(n, 4), rem(n, 4)
        blocks = [landed[pl.ds(pl.multiple_of((x * 32 + lt * 8 + g) * 8, 8), 8), :] for g in range(8)]
        blocks = block_transpose(blocks)
        for m in range(2):
            for var in range(4):
                result[pl.ds(lt * 256 + var * 64 + m * 4 + x, 8, stride=8), :] = blocks[m * 4 + var]
        return carry
    lax.fori_loop(0, 16, body, 0)


def shape(*dims, dtype=F32):
    return jax.ShapeDtypeStruct(dims, dtype)


def per_device(state, branch, obs_site, obs_value, patch_index, patch_weight):
    fields = state.reshape(ROWS, 8, WIDTH)
    dma = pltpu.SemaphoreType.DMA
    columns, table = pl.pallas_call(
        forecast_kernel,
        name="forecast",
        out_shape=[shape(MEM * 8, LANES), shape(MEM * 16, LANES)],
        in_specs=[VMEM] * 3,
        out_specs=[VMEM] * 2,
        scratch_shapes=[
            pltpu.VMEM((64, LANES), F32), pltpu.VMEM((64, LANES), F32),
            pltpu.VMEM((128, WIDTH), F32), pltpu.VMEM((128, WIDTH), F32),
            pltpu.VMEM((128, WIDTH), F32), pltpu.VMEM((128, WIDTH), F32),
            pltpu.VMEM((1024, LANES), F32), pltpu.VMEM((1024, LANES), F32), pltpu.VMEM((1024, LANES), F32),
            pltpu.VMEM((16, LANES), F32),
            dma((2,)), dma((2,)), dma((8,)), dma(()), dma(()), dma(()),
        ],
        compiler_params=pltpu.CompilerParams(collective_id=1, has_side_effects=True, vmem_limit_bytes=32 * 1024 * 1024),
    )(fields, branch, obs_site.reshape(8, LANES))
    outgoing = pl.pallas_call(
        analysis_kernel,
        name="analysis",
        out_shape=shape(MEM * 8, LANES),
        in_specs=[VMEM, VMEM, VMEM, ANY, VMEM],
        out_specs=VMEM,
        scratch_shapes=[
            pltpu.VMEM((COLS, LANES), jnp.int32), pltpu.VMEM((1024, LANES), F32), pltpu.VMEM((OBS, 2 * MEMBERS), BF16),
            pltpu.VMEM((LANES, LANES), F32), pltpu.VMEM((COLS, LANES), F32), pltpu.VMEM((1024, LANES), F32), dma(()),
        ],
        compiler_params=pltpu.CompilerParams(vmem_limit_bytes=32 * 1024 * 1024),
    )(columns, table, obs_value.reshape(8, LANES), patch_index, patch_weight.reshape(COLS, LANES))
    result = pl.pallas_call(
        return_kernel,
        name="return",
        out_shape=shape(1024, LANES),
        in_specs=[VMEM],
        out_specs=VMEM,
        scratch_shapes=[pltpu.VMEM((1024, LANES), F32), dma(()), dma(())],
        compiler_params=pltpu.CompilerParams(collective_id=2, has_side_effects=True, vmem_limit_bytes=32 * 1024 * 1024),
    )(outgoing)
    return result.reshape(4, ROWS, 2, 4, LANES).transpose(1, 2, 3, 0, 4).reshape(state.shape)


def solution(mesh):
    placed = (
        P(None, None, "mem", "tile", None),
        P(),
        P("tile", None),
        P("tile", None),
        P("tile", None, None),
        P("tile", "mem", None),
    )
    return jax.shard_map(
        per_device,
        mesh=mesh,
        in_specs=placed,
        out_specs=P(None, None, "mem", "tile", None),
        check_vma=False,
    )
```

```python
import jax
import jax.numpy as jnp
from jax import lax
from jax.experimental import pallas as pl
from jax.experimental.pallas import tpu as pltpu
from jax.sharding import PartitionSpec as P

MESH = pl.DeviceIdType.MESH
F32 = jnp.float32
BF16 = jnp.bfloat16
VMEM = pl.BlockSpec(memory_space=pltpu.VMEM)
ANY = pl.BlockSpec(memory_space=pl.ANY)
LEVELS, ROWS, WIDTH, LANES = 8, 32, 512, 128
MEM, COLS, MEMBERS, PATCH, OBS = 128, 16, 256, 128, 1024


def rem(a, b):
    return lax.rem(a, jnp.int32(b))


def div(a, b):
    return lax.div(a, jnp.int32(b))


def slot_of(device):
    core, y = rem(device, 2), rem(div(device, 2), 8)
    z, x = rem(div(device, 16), 2), div(device, 32)
    return core * 64 + x * 16 + y * 2 + z


def device_at(core, x, y, z):
    return x * 32 + z * 16 + y * 2 + core


def wait_rows(ref, sem, rows):
    part = ref.at[pl.ds(0, rows)]
    pltpu.make_async_copy(part, part, sem).wait()


def send(src, dst, send_sem, recv_sem, mem, tile):
    pltpu.make_async_remote_copy(
        src_ref=src, dst_ref=dst, send_sem=send_sem, recv_sem=recv_sem,
        device_id=(mem, tile), device_id_type=MESH,
    ).start()


def block_transpose(blocks):
    group = lax.broadcasted_iota(jnp.int32, (8, LANES), 1) // 16
    blocks = list(blocks)
    for bit in (1, 2, 4):
        upper = (group // bit) % 2 == 1
        for low in range(8):
            if low & bit:
                continue
            a, b = blocks[low], blocks[low + bit]
            blocks[low] = jnp.where(upper, pltpu.roll(b, 16 * bit, 1), a)
            blocks[low + bit] = jnp.where(upper, b, pltpu.roll(a, LANES - 16 * bit, 1))
    return blocks


def column_step(u, v, theta, energy, stab_m, stab_h):
    n = LEVELS
    km, kh, prod = [], [], []
    for k in range(n - 1):
        scale = 0.6 * jnp.sqrt(0.5 * (energy[k] + energy[k + 1]))
        km.append(scale * stab_m)
        kh.append(scale * stab_h)
        du, dv = u[k + 1] - u[k], v[k + 1] - v[k]
        prod.append(km[k] * (du * du + dv * dv))

    def solve(coef, extra, rhs):
        count = len(rhs)
        ratios, values = [], [[] for _ in range(count)]
        for k in range(n):
            pivot = 1.0 + extra[k] if extra is not None else 1.0
            if k > 0:
                pivot = pivot + coef[k - 1]
            if k < n - 1:
                pivot = pivot + coef[k]
            if k > 0:
                pivot = pivot - coef[k - 1] * ratios[-1]
            inverse = 1.0 / pivot
            for i in range(count):
                top = rhs[i][k]
                if k > 0:
                    top = top + coef[k - 1] * values[i][-1]
                values[i].append(top * inverse)
            if k < n - 1:
                ratios.append(coef[k] * inverse)
        out = []
        for i in range(count):
            result = [values[i][n - 1]]
            for k in range(n - 2, -1, -1):
                result.append(values[i][k] + ratios[k] * result[-1])
            out.append(result[::-1])
        return out

    source = []
    for k in range(n):
        if k == 0:
            total = prod[0]
        elif k == n - 1:
            total = prod[n - 2]
        else:
            total = prod[k - 1] + prod[k]
        source.append(energy[k] + 0.5 * total)
    sink = [0.3 * jnp.sqrt(energy[k]) for k in range(n)]
    new_u, new_v = solve(km, None, [u, v])
    (new_theta,) = solve(kh, None, [theta])
    (new_energy,) = solve(km, sink, [source])
    return new_u, new_v, new_theta, new_energy


def stabilities(branch):
    m = jnp.where(branch == 0, 0.25, jnp.where(branch == 1, 0.6, 1.2)).astype(F32)
    h = jnp.where(branch == 0, 0.15, jnp.where(branch == 1, 0.7, 1.6)).astype(F32)
    return m, h


def mix_columns(src, dst, stab_ref):
    def body(lt, carry):
        base = pl.multiple_of(lt * 256, 256)
        field = [[src[pl.ds(base + (var * 8 + k) * 8, 8), :] for k in range(LEVELS)] for var in range(4)]
        sbase = pl.multiple_of(lt * 16, 16)
        stab_m, stab_h = stab_ref[pl.ds(sbase, 8), :], stab_ref[pl.ds(sbase + 8, 8), :]
        new = column_step(*field, stab_m, stab_h)
        for var in range(4):
            for k in range(LEVELS):
                dst[pl.ds(base + (var * 8 + k) * 8, 8), :] = new[var][k]
        return carry
    lax.fori_loop(0, 4, body, 0)


def rows_of(ref, row):
    return jnp.broadcast_to(ref[pl.ds(row, 1), :], (8, WIDTH))


def laplace_step(centre, up, down):
    total = up + down + pltpu.roll(centre, 1, 1) + pltpu.roll(centre, WIDTH - 1, 1) - 4.0 * centre
    return centre + 0.2 * total


def put_tiles(dst, row, value):
    for lt in range(4):
        dst[pl.ds(pl.multiple_of(lt * 256 + row * 8, 8), 8), :] = value[:, lt * LANES:(lt + 1) * LANES]


def get_tiles(src, row):
    return jnp.concatenate(
        [src[pl.ds(pl.multiple_of(lt * 256 + row * 8, 8), 8), :] for lt in range(4)], axis=1)


def forecast_body(state, branch, stab, stab_edge, to_next, to_prev, from_prev, from_next, mixed, edge, halo_send, halo_recv, me, tile, rounds):
    sub = lax.broadcasted_iota(jnp.int32, (8, WIDTH), 0)
    next_tile, prev_tile = rem(tile + 1, 4), rem(tile + 3, 4)

    def pack(row, carry):
        for q, (n_sub, p_sub) in enumerate(((3, 0), (7, 4), (2, 1), (6, 5))):
            to_next[pl.ds(row * 4 + q, 1), :] = state[row, pl.ds(n_sub, 1), :]
            to_prev[pl.ds(row * 4 + q, 1), :] = state[row, pl.ds(p_sub, 1), :]
        return carry
    lax.fori_loop(0, ROWS, pack, 0)
    send(to_next, from_prev, halo_send.at[0], halo_recv.at[0], me, next_tile)
    send(to_prev, from_next, halo_send.at[1], halo_recv.at[1], me, prev_tile)

    own = [rows_of(branch, tile * 4 + x) for x in range(4)]
    before, after = rows_of(branch, rem(tile * 4 + 15, 16)), rows_of(branch, rem(tile * 4 + 4, 16))
    x_of = sub % 4
    own_rows = jnp.where(x_of == 0, own[0], jnp.where(x_of == 1, own[1], jnp.where(x_of == 2, own[2], own[3])))
    edge_rows = jnp.where(x_of < 2, before, after)
    for ref, rows in ((stab, own_rows), (stab_edge, edge_rows)):
        m, h = stabilities(rows)
        for lt in range(4):
            ref[pl.ds(lt * 16, 8), :] = m[:, lt * LANES:(lt + 1) * LANES]
            ref[pl.ds(lt * 16 + 8, 8), :] = h[:, lt * LANES:(lt + 1) * LANES]

    next(rounds)
    wait_rows(to_next, halo_send.at[0], 128)
    wait_rows(to_prev, halo_send.at[1], 128)
    wait_rows(from_prev, halo_recv.at[0], 128)
    wait_rows(from_next, halo_recv.at[1], 128)
    next(rounds)

    def pick(a, b, c, d):
        return jnp.where(x_of == 0, a, jnp.where(x_of == 1, b, jnp.where(x_of == 2, c, d)))

    def first(row, carry):
        centre = state[row]
        left = [rows_of(from_prev, row * 4 + q) for q in range(4)]
        right = [rows_of(from_next, row * 4 + q) for q in range(4)]
        up = jnp.where(x_of == 0, jnp.where(sub < 4, left[0], left[1]), pltpu.roll(centre, 1, 0))
        down = jnp.where(x_of == 3, jnp.where(sub < 4, right[0], right[1]), pltpu.roll(centre, 7, 0))
        put_tiles(mixed, row, laplace_step(centre, up, down))
        inner = [jnp.broadcast_to(state[row, pl.ds(s, 1), :], (8, WIDTH)) for s in (0, 4, 3, 7)]
        edge_centre = pick(left[0], left[1], right[0], right[1])
        outer = pick(left[2], left[3], right[2], right[3])
        put_tiles(edge, row, laplace_step(edge_centre, outer, pick(*inner)))
        return carry
    lax.fori_loop(0, ROWS, first, 0, unroll=4)
    mix_columns(mixed, mixed, stab)
    mix_columns(edge, edge, stab_edge)
    next(rounds)

    def second(row, carry):
        centre = get_tiles(mixed, row)
        sides = get_tiles(edge, row)
        side = [jnp.broadcast_to(sides[q:q + 1, :], (8, WIDTH)) for q in range(4)]
        up = jnp.where(x_of == 0, jnp.where(sub < 4, side[0], side[1]), pltpu.roll(centre, 1, 0))
        down = jnp.where(x_of == 3, jnp.where(sub < 4, side[2], side[3]), pltpu.roll(centre, 7, 0))
        put_tiles(mixed, row, laplace_step(centre, up, down))
        return carry
    lax.fori_loop(0, ROWS, second, 0, unroll=4)
    mix_columns(mixed, mixed, stab)


def observe(mixed, site, obs):
    sub = lax.broadcasted_iota(jnp.int32, (8, LANES), 0)
    sites = site[...]
    lane, x = sites % 128, (sites // 512) % 4
    key = (sites // 2048) * 4 + (sites // 128) % 4

    def spread(a, b):
        return jnp.broadcast_to(a[b:b + 1, :], (8, LANES))
    lanes = [spread(lane, b) for b in range(8)]
    keys = [spread(key, b) for b in range(8)]

    accs = []
    for b in range(8):
        def body(row, acc):
            for lt in range(4):
                tile = mixed[pl.ds(pl.multiple_of(lt * 256 + row * 8, 8), 8), :]
                found = jnp.take_along_axis(tile, lanes[b], axis=1, mode="promise_in_bounds")
                acc = jnp.where(keys[b] == row * 4 + lt, found, acc)
            return acc
        accs.append(lax.fori_loop(0, ROWS, body, jnp.zeros((8, LANES), F32), unroll=8))
    for b in range(8):
        only = jnp.where(sub % 4 == spread(x, b), accs[b], 0.0)
        only = only + pltpu.roll(only, 7, 0)
        only = only + pltpu.roll(only, 6, 0)
        obs[pl.ds(b, 1), :] = only[0:1, :]
        obs[pl.ds(8 + b, 1), :] = only[4:5, :]


def cut_columns(mixed, tiles):
    def body(n, carry):
        x, lt = div(n, 4), rem(n, 4)
        blocks = [mixed[pl.ds(lt * 256 + var * 64 + m * 4 + x, 8, stride=8), :] for m in range(2) for var in range(4)]
        for g, block in enumerate(block_transpose(blocks)):
            tiles[pl.ds(pl.multiple_of((x * 32 + lt * 8 + g) * 8, 8), 8), :] = block
        return carry
    lax.fori_loop(0, 16, body, 0, unroll=4)


def gather_obs(table, sems, me, tile):
    core, y, x = rem(me, 2), rem(div(me, 2), 8), div(me, 32)
    starts = (slot_of(me), core * 64 + x * 16 + y * 2, core * 64 + x * 16, core * 64)
    for n, (group, start, count) in enumerate(zip(near(me), starts, (1, 2, 16, 64))):
        rows = count * 16
        block = table.at[pl.ds(pl.multiple_of(start * 16, rows), rows)]
        for to in group:
            send(block, block, sems.at[2 * n], sems.at[2 * n + 1], to, tile)
        yield
        wait_rows(table, sems.at[2 * n], rows * len(group))
        wait_rows(table, sems.at[2 * n + 1], rows * len(group))


def near(me):
    core, y, z, x = rem(me, 2), rem(div(me, 2), 8), rem(div(me, 16), 2), div(me, 32)
    return (
        [device_at(core, x, y, 1 - z)],
        [device_at(core, x, rem(y + i, 8), z) for i in range(1, 8)],
        [device_at(core, rem(x + i, 4), y, z) for i in range(1, 4)],
        [device_at(1 - core, x, y, z)],
    )


def greet(me, tile):
    barrier = pltpu.get_barrier_semaphore()
    for step in (1, 3):
        pl.semaphore_signal(barrier, inc=1, device_id=(me, rem(tile + step, 4)), device_id_type=MESH)
    for group in near(me):
        for to in group:
            pl.semaphore_signal(barrier, inc=1, device_id=(to, tile), device_id_type=MESH)
    pl.semaphore_wait(barrier, 14)


def pass_on(arrived, me, tile):
    for n, group in enumerate(near(me)):
        for to in group:
            pl.semaphore_signal(arrived.at[n], inc=1, device_id=(to, tile), device_id_type=MESH)
        yield
        pl.semaphore_wait(arrived.at[n], len(group))


def split(a):
    high = a.astype(BF16)
    return high, (a - high.astype(F32)).astype(BF16)


def dot(a, b):
    return jnp.dot(a, b, preferred_element_type=F32)


def dot_t(a, b):
    return lax.dot_general(a, b, (((1,), (1,)), ((), ())), preferred_element_type=F32)


def dot3(a, pair):
    high, low = split(a)
    return dot(high, pair[0]) + (dot(low, pair[0]) + dot(high, pair[1]))


def prepare(table, value, index, weight, lookup, turned, gap):
    total = table[pl.ds(0, 16), :]
    total = lax.fori_loop(1, MEM, lambda s, t: t + table[pl.ds(pl.multiple_of(s * 16, 16), 16), :], total)
    mean = (total[:8] + total[8:]) * (1.0 / MEMBERS)
    diff = value[...] - mean
    for b in range(8):
        for m in range(2):
            block = table[pl.ds(m * 8 + b, MEM, stride=16), :] - mean[b:b + 1, :]
            high, low = split(jnp.transpose(block))
            lookup[pl.ds(b * 128, 128), pl.ds(m * 128, 128)] = high
            lookup[pl.ds(b * 128, 128), pl.ds(256 + m * 128, 128)] = low
    indices = index[...]
    both = jnp.concatenate([indices.astype(F32), weight[...], jnp.zeros((96, LANES), F32)], axis=0)
    turned[...] = jnp.transpose(both)
    for part in range(2):
        own = indices[part * 8:part * 8 + 8]
        found = jnp.zeros((8, LANES), F32)
        for b in range(8):
            row = jnp.broadcast_to(diff[b:b + 1, :], (8, LANES))
            taken = jnp.take_along_axis(row, own % 128, axis=1, mode="promise_in_bounds")
            found = jnp.where(own // 128 == b, taken, found)
        gap[pl.ds(part * 8, 8), :] = found


def eye():
    shape = (PATCH, PATCH)
    return (lax.broadcasted_iota(jnp.int32, shape, 0) == lax.broadcasted_iota(jnp.int32, shape, 1)).astype(F32)


def stacked(a):
    return jnp.concatenate(split(a), axis=0)


def beside(a):
    return jnp.concatenate(split(a), axis=1)


def folded(p, rows, width):
    return (p[:rows, :width] + p[rows:, :width]) + (p[:rows, width:] + p[rows:, width:])


GROUP = 4
BATCH = 4


def pick_obs(turned, lookup, picked):
    places = lax.broadcasted_iota(jnp.int32, (PATCH, OBS), 1)

    def body(n, carry):
        here = pltpu.roll(turned[...], LANES - n * GROUP, 1)
        chosen = [(places == here[:, i:i + 1].astype(jnp.int32)).astype(F32).astype(BF16) for i in range(GROUP)]
        rows = GROUP * PATCH
        found = dot(jnp.concatenate(chosen, axis=0), lookup[...])
        picked[pl.ds(pl.multiple_of(n * rows, rows), rows), :] = found.astype(BF16)
        return carry
    lax.fori_loop(0, COLS // GROUP, body, 0)


def patch_of(picked, c):
    return picked[pl.ds(pl.multiple_of(c * PATCH, PATCH), PATCH), :]


def sweep(turned, weight, picked, steps, turns, norms):
    def body(n, carry):
        one = eye()
        here = pltpu.roll(turned[...], LANES - n * BATCH, 1)
        cs = [n * BATCH + i for i in range(BATCH)]
        both = [patch_of(picked, c) for c in cs]
        both = [jnp.concatenate([p[:, :MEMBERS], p[:, MEMBERS:]], axis=0) for p in both]
        cov = [folded(dot_t(q, q), PATCH, PATCH) for q in both]
        cov_w = [v * (weight[pl.ds(c, 1), :] * (1.0 / (MEMBERS - 1.0))) for v, c in zip(cov, cs)]
        inv = []
        for i in range(BATCH):
            column = here[:, COLS + i:COLS + i + 1] * (1.0 / (MEMBERS - 1.0))
            total = jnp.sum(cov_w[i] * (2.0 * one + cov[i] * column), axis=0, keepdims=True)
            total = jnp.sum(total, axis=1, keepdims=True)
            inv.append(jnp.broadcast_to(1.0 / jnp.sqrt(MEMBERS + total), (1, PATCH)))
        step = [(one + v) * t for v, t in zip(cov_w, inv)]
        parts = [split(k) for k in step]
        wide = [jnp.concatenate(p, axis=1) for p in parts]
        square = [folded(dot(jnp.concatenate(p, axis=0), k), PATCH, PATCH) for p, k in zip(parts, wide)]
        inner = [2.25 * one - 1.5 * k + 0.25 * q for k, q in zip(step, square)]
        turn = [folded(dot(stacked(g), k), PATCH, PATCH) for g, k in zip(inner, wide)]
        for i, c in enumerate(cs):
            here_rows = pl.ds(pl.multiple_of(c * PATCH, PATCH), PATCH)
            steps[here_rows, :] = wide[i]
            turns[here_rows, :] = beside(turn[i])
            norms[pl.ds(c, 1), :] = inv[i]
        return carry
    lax.fori_loop(0, COLS // BATCH, body, 0)


def apply(fields, weight, gap, picked, steps, turns, norms, analysed):
    def body(n, carry):
        cs = [n * BATCH + i for i in range(BATCH)]
        todo = range(BATCH)
        first_row = lax.broadcasted_iota(jnp.int32, (16, PATCH), 0) == 0
        zeros = jnp.zeros((16, PATCH), F32)
        x = []
        for c in cs:
            parts = [fields[pl.ds((m * 4 + var) * 16 + c, 8, stride=128), :] for m in range(2) for var in range(4)]
            x.append(jnp.concatenate([jnp.concatenate(parts[:4], axis=0), jnp.concatenate(parts[4:], axis=0)], axis=1))
        mean = [jnp.sum(a, axis=1, keepdims=True) * (1.0 / MEMBERS) for a in x]
        pert = [a - b for a, b in zip(x, mean)]
        patch = [patch_of(picked, c) for c in cs]
        w = [weight[pl.ds(c, 1), :] for c in cs]
        inv = [norms[pl.ds(c, 1), :] for c in cs]
        cross = []
        for i in todo:
            p = jnp.concatenate([patch[i][:, :MEMBERS], patch[i][:, MEMBERS:]], axis=0)
            cross.append(folded(dot_t(stacked(pert[i]), p), ROWS, PATCH) * (w[i] * inv[i] * (1.0 / (MEMBERS - 1.0))))
        force = [jnp.where(first_row, w[i] * gap[pl.ds(c, 1), :], 0.0) for i, c in enumerate(cs)]
        step = [patch_of(steps, c) for c in cs]
        once = [folded(dot(stacked(jnp.concatenate([cross[i], force[i]], axis=0)), step[i]), 48, PATCH) for i in todo]
        twice = [folded(dot(stacked(once[i][:ROWS]), step[i]), ROWS, PATCH) for i in todo]
        turn = [patch_of(turns, c) for c in cs]
        v, a, u, t1 = [], [], [], []
        for i in todo:
            t = inv[i]
            a0, a1 = 2.25 - 1.5 * t + 0.25 * t * t, 0.25 * t - 1.5
            v.append(jnp.concatenate([a0 * cross[i] + a1 * once[i][:ROWS] + 0.25 * twice[i], zeros], axis=0))
            t1.append(t * a0)
            a.append(1.5 - 0.5 * t)
            u.append(jnp.concatenate([-0.5 * cross[i], 1.5 * force[i] - 0.5 * once[i][ROWS:]], axis=0))

        def times_t1(a, u):
            new = [folded(dot(stacked(u[i]), turn[i]), 48, PATCH) + a[i] * v[i] for i in todo]
            return [a[i] * t1[i] for i in todo], new

        def times_f1(a, u):
            a2, u2 = times_t1(a, u)
            return [1.5 * a[i] - 0.5 * a2[i] for i in todo], [1.5 * u[i] - 0.5 * u2[i] for i in todo]
        a, u = times_f1(a, u)
        a2, u2 = times_f1(*times_f1(*times_t1(a, u)))
        a = [1.5 * a[i] - 0.5 * a2[i] for i in todo]
        u = [1.5 * u[i] - 0.5 * u2[i] for i in todo]
        spread = [folded(dot(stacked(u[i]), patch[i]), 48, MEMBERS) for i in todo]
        for i, c in enumerate(cs):
            scale = jnp.sqrt(inv[i])
            scale = jnp.concatenate([scale, scale], axis=1)
            share = jnp.concatenate([a[i], a[i]], axis=1)
            moved = (share * pert[i] + spread[i][:ROWS]) * scale
            nudge = spread[i][ROWS:ROWS + 1] * scale
            out = moved + (mean[i] + jnp.sum(moved * nudge, axis=1, keepdims=True) * (1.0 / (MEMBERS - 1.0)))
            for m in range(2):
                for var in range(4):
                    analysed[pl.ds((m * 4 + var) * 16 + c, 8, stride=128), :] = out[var * 8:var * 8 + 8, m * 128:m * 128 + 128]
        return carry
    lax.fori_loop(0, COLS // BATCH, body, 0)


def turn_members(src, dst):
    for level in range(LEVELS):
        dst[pl.ds(level * 128, 128), :] = jnp.transpose(src[pl.ds(level, MEM, stride=8), :])


def turn_back(src, dst):
    for level in range(LEVELS):
        dst[pl.ds(level, MEM, stride=8), :] = jnp.transpose(src[pl.ds(level * 128, 128), :])


def kernel(state, branch, site, value, index_all, weight, result,
           stab, stab_edge, to_next, to_prev, from_prev, from_next, mixed, edge, tiles, columns, obs, table,
           index, fields, lookup, turned, gap, analysed, picked, steps, turns, norms, outgoing, landed,
           halo_send, halo_recv, gather_sems, out_sems, in_sems, index_sem, arrived):
    me, tile = lax.axis_index("mem"), lax.axis_index("tile")
    greet(me, tile)
    rounds = pass_on(arrived, me, tile)
    next(rounds)
    fetch = pltpu.make_async_copy(index_all.at[0, pl.ds(pl.multiple_of(me * COLS, COLS), COLS)], index, index_sem)
    fetch.start()
    forecast_body(state, branch, stab, stab_edge, to_next, to_prev, from_prev, from_next, mixed, edge, halo_send, halo_recv, me, tile, rounds)
    slot = slot_of(me)
    here = pl.ds(pl.multiple_of(slot * 8, 8), 8)

    def send_columns():
        def body(i, carry):
            to = rem(me + i, MEM)
            send(tiles.at[pl.ds(pl.multiple_of(to * 8, 8), 8)], columns.at[here], out_sems.at[0], in_sems.at[0], to, tile)
            return carry
        lax.fori_loop(1, MEM, body, 0)
        columns[here, :] = tiles[pl.ds(pl.multiple_of(me * 8, 8), 8), :]

    observe(mixed, site, obs)
    table[pl.ds(pl.multiple_of(slot * 16, 16), 16), :] = obs[...]
    gather = gather_obs(table, gather_sems, me, tile)
    next(gather)
    cut_columns(mixed, tiles)
    for _ in rounds:
        pass
    next(gather)
    if ORDER == 0:
        send_columns()
        next(gather)
        next(gather)
    elif ORDER == 1:
        next(gather)
        send_columns()
        next(gather)
    else:
        next(gather)
        next(gather)
        send_columns()
    for _ in gather:
        pass
    fetch.wait()
    prepare(table, value, index, weight, lookup, turned, gap)
    pick_obs(turned, lookup, picked)
    sweep(turned, weight, picked, steps, turns, norms)
    wait_rows(tiles, out_sems.at[0], 8 * (MEM - 1))
    wait_rows(columns, in_sems.at[0], 8 * (MEM - 1))
    turn_members(columns, fields)
    apply(fields, weight, gap, picked, steps, turns, norms, analysed)
    turn_back(analysed, outgoing)
    mine = pl.ds(pl.multiple_of(me * 8, 8), 8)

    def give_back(i, carry):
        to = rem(me + i, MEM)
        send(outgoing.at[pl.ds(pl.multiple_of(slot_of(to) * 8, 8), 8)], landed.at[mine], out_sems.at[1], in_sems.at[1], to, tile)
        return carry
    lax.fori_loop(1, MEM, give_back, 0)
    landed[mine, :] = outgoing[here, :]
    wait_rows(outgoing, out_sems.at[1], 8 * (MEM - 1))
    wait_rows(landed, in_sems.at[1], 8 * (MEM - 1))
    place(landed, result)


ORDER = 0


def place(landed, result):
    def body(n, carry):
        x, lt = div(n, 4), rem(n, 4)
        blocks = [landed[pl.ds(pl.multiple_of((x * 32 + lt * 8 + g) * 8, 8), 8), :] for g in range(8)]
        blocks = block_transpose(blocks)
        for m in range(2):
            for var in range(4):
                result[pl.ds(lt * 256 + var * 64 + m * 4 + x, 8, stride=8), :] = blocks[m * 4 + var]
        return carry
    lax.fori_loop(0, 16, body, 0, unroll=4)


def shape(*dims, dtype=F32):
    return jax.ShapeDtypeStruct(dims, dtype)


def per_device(state, branch, obs_site, obs_value, patch_index, patch_weight):
    fields = state.reshape(ROWS, 8, WIDTH)
    dma = pltpu.SemaphoreType.DMA
    regular = pltpu.SemaphoreType.REGULAR

    def rows(n, width=LANES, dtype=F32):
        return pltpu.VMEM((n, width), dtype)
    result = pl.pallas_call(
        kernel,
        name="forecast_analysis",
        out_shape=shape(1024, LANES),
        in_specs=[VMEM, VMEM, VMEM, VMEM, ANY, VMEM],
        out_specs=VMEM,
        scratch_shapes=[
            rows(64), rows(64), rows(128, WIDTH), rows(128, WIDTH), rows(128, WIDTH), rows(128, WIDTH),
            rows(1024), rows(1024), rows(1024), rows(1024), rows(16), rows(MEM * 16),
            rows(COLS, LANES, jnp.int32), rows(1024), rows(OBS, 2 * MEMBERS, BF16), rows(LANES), rows(COLS), rows(1024),
            rows(COLS * PATCH, 2 * MEMBERS, BF16), rows(COLS * PATCH, 2 * PATCH, BF16), rows(COLS * PATCH, 2 * PATCH, BF16),
            rows(COLS), rows(1024), rows(1024),
            dma((2,)), dma((2,)), dma((8,)), dma((2,)), dma((2,)), dma(()), regular((4,)),
        ],
        compiler_params=pltpu.CompilerParams(collective_id=1, has_side_effects=True, vmem_limit_bytes=40 * 1024 * 1024),
    )(fields, branch, obs_site.reshape(8, LANES), obs_value.reshape(8, LANES), patch_index, patch_weight.reshape(COLS, LANES))
    return result.reshape(4, ROWS, 2, 4, LANES).transpose(1, 2, 3, 0, 4).reshape(state.shape)


def solution(mesh):
    placed = (
        P(None, None, "mem", "tile", None),
        P(),
        P("tile", None),
        P("tile", None),
        P("tile", None, None),
        P("tile", "mem", None),
    )
    return jax.shard_map(
        per_device,
        mesh=mesh,
        in_specs=placed,
        out_specs=P(None, None, "mem", "tile", None),
        check_vma=False,
    )
```

```python
import jax
import jax.numpy as jnp
from jax import lax
from jax.experimental import pallas as pl
from jax.experimental.pallas import tpu as pltpu
from jax.sharding import PartitionSpec as P

MESH = pl.DeviceIdType.MESH
F32 = jnp.float32
BF16 = jnp.bfloat16
VMEM = pl.BlockSpec(memory_space=pltpu.VMEM)
HBM = pl.BlockSpec(memory_space=pltpu.HBM)
LEVELS, ROWS, WIDTH, LANES = 8, 32, 512, 128
MEM, COLS, MEMBERS, PATCH, OBS = 128, 16, 256, 128, 1024


def rem(a, b):
    return lax.rem(a, jnp.int32(b))


def div(a, b):
    return lax.div(a, jnp.int32(b))


def slot_of(device):
    core, y = rem(device, 2), rem(div(device, 2), 8)
    z, x = rem(div(device, 16), 2), div(device, 32)
    return core * 64 + x * 16 + y * 2 + z


def device_at(core, x, y, z):
    return x * 32 + z * 16 + y * 2 + core


def wait_rows(ref, sem, rows):
    part = ref.at[pl.ds(0, rows)]
    pltpu.make_async_copy(part, part, sem).wait()


def send(src, dst, send_sem, recv_sem, mem, tile):
    pltpu.make_async_remote_copy(
        src_ref=src, dst_ref=dst, send_sem=send_sem, recv_sem=recv_sem,
        device_id=(mem, tile), device_id_type=MESH,
    ).start()


def block_transpose(blocks):
    group = lax.broadcasted_iota(jnp.int32, (8, LANES), 1) // 16
    blocks = list(blocks)
    for bit in (1, 2, 4):
        upper = (group // bit) % 2 == 1
        for low in range(8):
            if low & bit:
                continue
            a, b = blocks[low], blocks[low + bit]
            blocks[low] = jnp.where(upper, pltpu.roll(b, 16 * bit, 1), a)
            blocks[low + bit] = jnp.where(upper, b, pltpu.roll(a, LANES - 16 * bit, 1))
    return blocks


def column_step(u, v, theta, energy, stab_m, stab_h):
    n = LEVELS
    km, kh, prod = [], [], []
    for k in range(n - 1):
        scale = 0.6 * jnp.sqrt(0.5 * (energy[k] + energy[k + 1]))
        km.append(scale * stab_m)
        kh.append(scale * stab_h)
        du, dv = u[k + 1] - u[k], v[k + 1] - v[k]
        prod.append(km[k] * (du * du + dv * dv))

    def solve(coef, extra, rhs):
        count = len(rhs)
        ratios, values = [], [[] for _ in range(count)]
        for k in range(n):
            pivot = 1.0 + extra[k] if extra is not None else 1.0
            if k > 0:
                pivot = pivot + coef[k - 1]
            if k < n - 1:
                pivot = pivot + coef[k]
            if k > 0:
                pivot = pivot - coef[k - 1] * ratios[-1]
            inverse = 1.0 / pivot
            for i in range(count):
                top = rhs[i][k]
                if k > 0:
                    top = top + coef[k - 1] * values[i][-1]
                values[i].append(top * inverse)
            if k < n - 1:
                ratios.append(coef[k] * inverse)
        out = []
        for i in range(count):
            result = [values[i][n - 1]]
            for k in range(n - 2, -1, -1):
                result.append(values[i][k] + ratios[k] * result[-1])
            out.append(result[::-1])
        return out

    source = []
    for k in range(n):
        if k == 0:
            total = prod[0]
        elif k == n - 1:
            total = prod[n - 2]
        else:
            total = prod[k - 1] + prod[k]
        source.append(energy[k] + 0.5 * total)
    sink = [0.3 * jnp.sqrt(energy[k]) for k in range(n)]
    new_u, new_v = solve(km, None, [u, v])
    (new_theta,) = solve(kh, None, [theta])
    (new_energy,) = solve(km, sink, [source])
    return new_u, new_v, new_theta, new_energy


def stabilities(branch):
    m = jnp.where(branch == 0, 0.25, jnp.where(branch == 1, 0.6, 1.2)).astype(F32)
    h = jnp.where(branch == 0, 0.15, jnp.where(branch == 1, 0.7, 1.6)).astype(F32)
    return m, h


def mix_columns(src, dst, stab_ref):
    def body(lt, carry):
        base = pl.multiple_of(lt * 256, 256)
        field = [[src[pl.ds(base + (var * 8 + k) * 8, 8), :] for k in range(LEVELS)] for var in range(4)]
        sbase = pl.multiple_of(lt * 16, 16)
        stab_m, stab_h = stab_ref[pl.ds(sbase, 8), :], stab_ref[pl.ds(sbase + 8, 8), :]
        new = column_step(*field, stab_m, stab_h)
        for var in range(4):
            for k in range(LEVELS):
                dst[pl.ds(base + (var * 8 + k) * 8, 8), :] = new[var][k]
        return carry
    lax.fori_loop(0, 4, body, 0)


def rows_of(ref, row):
    return jnp.broadcast_to(ref[pl.ds(row, 1), :], (8, WIDTH))


def laplace_step(centre, up, down):
    total = up + down + pltpu.roll(centre, 1, 1) + pltpu.roll(centre, WIDTH - 1, 1) - 4.0 * centre
    return centre + 0.2 * total


def put_tiles(dst, row, value):
    for lt in range(4):
        dst[pl.ds(pl.multiple_of(lt * 256 + row * 8, 8), 8), :] = value[:, lt * LANES:(lt + 1) * LANES]


def get_tiles(src, row):
    return jnp.concatenate(
        [src[pl.ds(pl.multiple_of(lt * 256 + row * 8, 8), 8), :] for lt in range(4)], axis=1)


def forecast_body(state, branch, stab, stab_edge, to_next, to_prev, from_prev, from_next, mixed, edge, halo_send, halo_recv, me, tile, greeting, rounds, state_here, branch_here):
    sub = lax.broadcasted_iota(jnp.int32, (8, WIDTH), 0)
    next_tile, prev_tile = rem(tile + 1, 4), rem(tile + 3, 4)
    state_here()

    def pack(row, carry):
        for q, (n_sub, p_sub) in enumerate(((3, 0), (7, 4), (2, 1), (6, 5))):
            to_next[pl.ds(row * 4 + q, 1), :] = state[row, pl.ds(n_sub, 1), :]
            to_prev[pl.ds(row * 4 + q, 1), :] = state[row, pl.ds(p_sub, 1), :]
        return carry
    lax.fori_loop(0, ROWS, pack, 0, unroll=4)
    for _ in greeting:
        pass
    for var in range(4):
        rows = pl.ds(var * 32, 32)
        send(to_next.at[rows], from_prev.at[rows], halo_send.at[0], halo_recv.at[var], me, next_tile)
        send(to_prev.at[rows], from_next.at[rows], halo_send.at[1], halo_recv.at[4 + var], me, prev_tile)
    next(rounds)

    branch_here()
    own = [rows_of(branch, tile * 4 + x) for x in range(4)]
    before, after = rows_of(branch, rem(tile * 4 + 15, 16)), rows_of(branch, rem(tile * 4 + 4, 16))
    x_of = sub % 4
    own_rows = jnp.where(x_of == 0, own[0], jnp.where(x_of == 1, own[1], jnp.where(x_of == 2, own[2], own[3])))
    edge_rows = jnp.where(x_of < 2, before, after)
    for ref, rows in ((stab, own_rows), (stab_edge, edge_rows)):
        m, h = stabilities(rows)
        for lt in range(4):
            ref[pl.ds(lt * 16, 8), :] = m[:, lt * LANES:(lt + 1) * LANES]
            ref[pl.ds(lt * 16 + 8, 8), :] = h[:, lt * LANES:(lt + 1) * LANES]
    next(rounds)

    def pick(a, b, c, d):
        return jnp.where(x_of == 0, a, jnp.where(x_of == 1, b, jnp.where(x_of == 2, c, d)))

    def first(row, carry):
        centre = state[row]
        left = [rows_of(from_prev, row * 4 + q) for q in range(4)]
        right = [rows_of(from_next, row * 4 + q) for q in range(4)]
        up = jnp.where(x_of == 0, jnp.where(sub < 4, left[0], left[1]), pltpu.roll(centre, 1, 0))
        down = jnp.where(x_of == 3, jnp.where(sub < 4, right[0], right[1]), pltpu.roll(centre, 7, 0))
        put_tiles(mixed, row, laplace_step(centre, up, down))
        inner = [jnp.broadcast_to(state[row, pl.ds(s, 1), :], (8, WIDTH)) for s in (0, 4, 3, 7)]
        edge_centre = pick(left[0], left[1], right[0], right[1])
        outer = pick(left[2], left[3], right[2], right[3])
        put_tiles(edge, row, laplace_step(edge_centre, outer, pick(*inner)))
        return carry
    for var in range(4):
        wait_rows(from_prev, halo_recv.at[var], 32)
        wait_rows(from_next, halo_recv.at[4 + var], 32)
        lax.fori_loop(var * 8, var * 8 + 8, first, 0, unroll=4)
    mix_columns(mixed, mixed, stab)
    mix_columns(edge, edge, stab_edge)
    next(rounds)

    def second(row, carry):
        centre = get_tiles(mixed, row)
        sides = get_tiles(edge, row)
        side = [jnp.broadcast_to(sides[q:q + 1, :], (8, WIDTH)) for q in range(4)]
        up = jnp.where(x_of == 0, jnp.where(sub < 4, side[0], side[1]), pltpu.roll(centre, 1, 0))
        down = jnp.where(x_of == 3, jnp.where(sub < 4, side[2], side[3]), pltpu.roll(centre, 7, 0))
        put_tiles(mixed, row, laplace_step(centre, up, down))
        return carry
    lax.fori_loop(0, ROWS, second, 0, unroll=4)
    mix_columns(mixed, mixed, stab)
    wait_rows(to_next, halo_send.at[0], 128)
    wait_rows(to_prev, halo_send.at[1], 128)


def observe(mixed, site, obs):
    sub = lax.broadcasted_iota(jnp.int32, (8, LANES), 0)
    sites = site[...]
    lane, x = sites % 128, (sites // 512) % 4
    key = (sites // 2048) * 4 + (sites // 128) % 4

    def spread(a, b):
        return jnp.broadcast_to(a[b:b + 1, :], (8, LANES))
    lanes = [spread(lane, b) for b in range(8)]
    keys = [spread(key, b) for b in range(8)]

    accs = []
    for b in range(8):
        def body(row, acc):
            for lt in range(4):
                tile = mixed[pl.ds(pl.multiple_of(lt * 256 + row * 8, 8), 8), :]
                found = jnp.take_along_axis(tile, lanes[b], axis=1, mode="promise_in_bounds")
                acc = jnp.where(keys[b] == row * 4 + lt, found, acc)
            return acc
        accs.append(lax.fori_loop(0, ROWS, body, jnp.zeros((8, LANES), F32), unroll=8))
    for b in range(8):
        only = jnp.where(sub % 4 == spread(x, b), accs[b], 0.0)
        only = only + pltpu.roll(only, 7, 0)
        only = only + pltpu.roll(only, 6, 0)
        obs[pl.ds(b, 1), :] = only[0:1, :]
        obs[pl.ds(8 + b, 1), :] = only[4:5, :]


def cut_columns(mixed, tiles):
    def body(n, carry):
        x, lt = div(n, 4), rem(n, 4)
        blocks = [mixed[pl.ds(lt * 256 + var * 64 + m * 4 + x, 8, stride=8), :] for m in range(2) for var in range(4)]
        for g, block in enumerate(block_transpose(blocks)):
            tiles[pl.ds(pl.multiple_of((x * 32 + lt * 8 + g) * 8, 8), 8), :] = block
        return carry
    lax.fori_loop(0, 16, body, 0, unroll=4)


def gather_obs(table, send_sems, plane_sems, x_sems, core_sem, me, tile):
    core, y, z, x = rem(me, 2), rem(div(me, 2), 8), rem(div(me, 16), 2), div(me, 32)

    def part(first, count):
        return table.at[pl.ds(pl.multiple_of(first * 16, count * 16), count * 16)]

    def slot(y_of, z_of):
        return part(core * 64 + x * 16 + y_of * 2 + z_of, 1)

    def pass_slot(one):
        for j in (2, 1, 3):
            send(one, one, send_sems.at[1], x_sems.at[j - 1], device_at(core, rem(x + j, 4), y, z), tile)
        send(one, one, send_sems.at[2], core_sem, device_at(1 - core, x, y, z), tile)
    own = slot(y, z)
    for i in (4, 3, 5, 2, 6, 1, 7, 0):
        send(own, own, send_sems.at[0], plane_sems.at[7 + i], device_at(core, x, rem(y + i, 8), 1 - z), tile)
        if i:
            send(own, own, send_sems.at[0], plane_sems.at[i - 1], device_at(core, x, rem(y + i, 8), z), tile)
    pass_slot(own)
    yield
    for i in (1, 7, 2, 6, 3, 5, 4):
        wait_rows(table, plane_sems.at[i - 1], 16)
        pass_slot(slot(rem(y + 8 - i, 8), z))
    for i in (0, 1, 7, 2, 6, 3, 5, 4):
        wait_rows(table, plane_sems.at[7 + i], 16)
        pass_slot(slot(rem(y + 8 - i, 8), 1 - z))
    yield
    for j in (1, 3, 2):
        wait_rows(table, x_sems.at[j - 1], 256)
        plane = part(core * 64 + rem(x + 4 - j, 4) * 16, 16)
        send(plane, plane, send_sems.at[2], core_sem, device_at(1 - core, x, y, z), tile)
    wait_rows(table, core_sem, 1024)
    wait_rows(table, send_sems.at[0], 16 * 15)
    wait_rows(table, send_sems.at[1], 256 * 3)
    wait_rows(table, send_sems.at[2], 1024)


def each_device(me, do):
    core, y, z, x = rem(me, 2), rem(div(me, 2), 8), rem(div(me, 16), 2), div(me, 32)

    def all_at(y_to, z_to, own):
        for i in (2, 1, 3, 0):
            for c in (1, 0):
                if not (own and i == 0 and c == 0):
                    do(device_at(rem(core + c, 2), rem(x + i, 4), y_to, z_to))

    def far(n, carry):
        half = div(n + 1, 2)
        step = rem(12 + (2 * rem(n, 2) - 1) * half, 8)
        all_at(rem(y + step, 8), 1 - z, False)
        return carry

    def close(n, carry):
        half = div(n + 1, 2)
        step = rem(12 + (2 * rem(n, 2) - 1) * half, 8)
        all_at(rem(y + step, 8), z, False)
        return carry
    lax.fori_loop(0, 8, far, 0)
    lax.fori_loop(0, 7, close, 0)
    all_at(y, z, True)


def near(me):
    core, y, z, x = rem(me, 2), rem(div(me, 2), 8), rem(div(me, 16), 2), div(me, 32)
    return (
        [device_at(core, x, rem(y + i, 8), z) for i in range(1, 8)] + [device_at(core, x, rem(y + i, 8), 1 - z) for i in range(8)],
        [device_at(core, rem(x + i, 4), y, z) for i in range(1, 4)],
        [device_at(1 - core, x, y, z)],
    )


def greet(me, tile):
    barrier = pltpu.get_barrier_semaphore()
    for step in (1, 3):
        pl.semaphore_signal(barrier, inc=1, device_id=(me, rem(tile + step, 4)), device_id_type=MESH)
    for group in near(me):
        for to in group:
            pl.semaphore_signal(barrier, inc=1, device_id=(to, tile), device_id_type=MESH)
    yield
    pl.semaphore_wait(barrier, 2 + 15 + 3 + 1)


def pass_on(arrived, me, tile):
    for n, group in enumerate(near(me)):
        for to in group:
            pl.semaphore_signal(arrived.at[n], inc=1, device_id=(to, tile), device_id_type=MESH)
        yield
        pl.semaphore_wait(arrived.at[n], len(group))


def split(a):
    high = a.astype(BF16)
    return high, (a - high.astype(F32)).astype(BF16)


def dot(a, b):
    return jnp.dot(a, b, preferred_element_type=F32)


def dot_t(a, b):
    return lax.dot_general(a, b, (((1,), (1,)), ((), ())), preferred_element_type=F32)


def dot3(a, pair):
    high, low = split(a)
    return dot(high, pair[0]) + (dot(low, pair[0]) + dot(high, pair[1]))


def prepare(table, value, index, weight, lookup, turned, gap):
    total = table[pl.ds(0, 16), :]
    total = lax.fori_loop(1, MEM, lambda s, t: t + table[pl.ds(pl.multiple_of(s * 16, 16), 16), :], total)
    mean = (total[:8] + total[8:]) * (1.0 / MEMBERS)
    diff = value[...] - mean
    for b in range(8):
        for m in range(2):
            block = table[pl.ds(m * 8 + b, MEM, stride=16), :] - mean[b:b + 1, :]
            high, low = split(jnp.transpose(block))
            lookup[pl.ds(b * 128, 128), pl.ds(m * 128, 128)] = high
            lookup[pl.ds(b * 128, 128), pl.ds(256 + m * 128, 128)] = low
    indices = index[...]
    both = jnp.concatenate([indices.astype(F32), weight[...], jnp.zeros((96, LANES), F32)], axis=0)
    turned[...] = jnp.transpose(both)
    for part in range(2):
        own = indices[part * 8:part * 8 + 8]
        found = jnp.zeros((8, LANES), F32)
        for b in range(8):
            row = jnp.broadcast_to(diff[b:b + 1, :], (8, LANES))
            taken = jnp.take_along_axis(row, own % 128, axis=1, mode="promise_in_bounds")
            found = jnp.where(own // 128 == b, taken, found)
        gap[pl.ds(part * 8, 8), :] = found


def eye():
    shape = (PATCH, PATCH)
    return (lax.broadcasted_iota(jnp.int32, shape, 0) == lax.broadcasted_iota(jnp.int32, shape, 1)).astype(F32)


def stacked(a):
    return jnp.concatenate(split(a), axis=0)


def beside(a):
    return jnp.concatenate(split(a), axis=1)


def folded(p, rows, width):
    return (p[:rows, :width] + p[rows:, :width]) + (p[:rows, width:] + p[rows:, width:])


GROUP = 4
BATCH = 4


def pick_obs(turned, lookup, picked):
    places = lax.broadcasted_iota(jnp.int32, (PATCH, OBS), 1)

    def body(n, carry):
        here = pltpu.roll(turned[...], LANES - n * GROUP, 1)
        chosen = [(places == here[:, i:i + 1].astype(jnp.int32)).astype(F32).astype(BF16) for i in range(GROUP)]
        rows = GROUP * PATCH
        found = dot(jnp.concatenate(chosen, axis=0), lookup[...])
        picked[pl.ds(pl.multiple_of(n * rows, rows), rows), :] = found.astype(BF16)
        return carry
    lax.fori_loop(0, COLS // GROUP, body, 0)


def patch_of(picked, c):
    return picked[pl.ds(pl.multiple_of(c * PATCH, PATCH), PATCH), :]


def sweep(turned, weight, picked, steps, turns, norms):
    def body(n, carry):
        one = eye()
        here = pltpu.roll(turned[...], LANES - n * BATCH, 1)
        cs = [n * BATCH + i for i in range(BATCH)]
        both = [patch_of(picked, c) for c in cs]
        both = [jnp.concatenate([p[:, :MEMBERS], p[:, MEMBERS:]], axis=0) for p in both]
        cov = [folded(dot_t(q, q), PATCH, PATCH) for q in both]
        cov_w = [v * (weight[pl.ds(c, 1), :] * (1.0 / (MEMBERS - 1.0))) for v, c in zip(cov, cs)]
        inv = []
        for i in range(BATCH):
            column = here[:, COLS + i:COLS + i + 1] * (1.0 / (MEMBERS - 1.0))
            total = jnp.sum(cov_w[i] * (2.0 * one + cov[i] * column), axis=0, keepdims=True)
            total = jnp.sum(total, axis=1, keepdims=True)
            inv.append(jnp.broadcast_to(1.0 / jnp.sqrt(MEMBERS + total), (1, PATCH)))
        step = [(one + v) * t for v, t in zip(cov_w, inv)]
        parts = [split(k) for k in step]
        wide = [jnp.concatenate(p, axis=1) for p in parts]
        square = [folded(dot(jnp.concatenate(p, axis=0), k), PATCH, PATCH) for p, k in zip(parts, wide)]
        inner = [2.25 * one - 1.5 * k + 0.25 * q for k, q in zip(step, square)]
        turn = [folded(dot(stacked(g), k), PATCH, PATCH) for g, k in zip(inner, wide)]
        for i, c in enumerate(cs):
            here_rows = pl.ds(pl.multiple_of(c * PATCH, PATCH), PATCH)
            steps[here_rows, :] = wide[i]
            turns[here_rows, :] = beside(turn[i])
            norms[pl.ds(c, 1), :] = inv[i]
        return carry
    lax.fori_loop(0, COLS // BATCH, body, 0)


def apply(fields, weight, gap, picked, steps, turns, norms, analysed):
    def body(n, carry):
        cs = [n * BATCH + i for i in range(BATCH)]
        todo = range(BATCH)
        first_row = lax.broadcasted_iota(jnp.int32, (16, PATCH), 0) == 0
        zeros = jnp.zeros((16, PATCH), F32)
        x = []
        for c in cs:
            parts = [fields[pl.ds((m * 4 + var) * 16 + c, 8, stride=128), :] for m in range(2) for var in range(4)]
            x.append(jnp.concatenate([jnp.concatenate(parts[:4], axis=0), jnp.concatenate(parts[4:], axis=0)], axis=1))
        mean = [jnp.sum(a, axis=1, keepdims=True) * (1.0 / MEMBERS) for a in x]
        pert = [a - b for a, b in zip(x, mean)]
        patch = [patch_of(picked, c) for c in cs]
        w = [weight[pl.ds(c, 1), :] for c in cs]
        inv = [norms[pl.ds(c, 1), :] for c in cs]
        cross = []
        for i in todo:
            p = jnp.concatenate([patch[i][:, :MEMBERS], patch[i][:, MEMBERS:]], axis=0)
            cross.append(folded(dot_t(stacked(pert[i]), p), ROWS, PATCH) * (w[i] * inv[i] * (1.0 / (MEMBERS - 1.0))))
        force = [jnp.where(first_row, w[i] * gap[pl.ds(c, 1), :], 0.0) for i, c in enumerate(cs)]
        step = [patch_of(steps, c) for c in cs]
        once = [folded(dot(stacked(jnp.concatenate([cross[i], force[i]], axis=0)), step[i]), 48, PATCH) for i in todo]
        twice = [folded(dot(stacked(once[i][:ROWS]), step[i]), ROWS, PATCH) for i in todo]
        turn = [patch_of(turns, c) for c in cs]
        v, a, u, t1 = [], [], [], []
        for i in todo:
            t = inv[i]
            a0, a1 = 2.25 - 1.5 * t + 0.25 * t * t, 0.25 * t - 1.5
            v.append(jnp.concatenate([a0 * cross[i] + a1 * once[i][:ROWS] + 0.25 * twice[i], zeros], axis=0))
            t1.append(t * a0)
            a.append(1.5 - 0.5 * t)
            u.append(jnp.concatenate([-0.5 * cross[i], 1.5 * force[i] - 0.5 * once[i][ROWS:]], axis=0))

        def times_t1(a, u):
            new = [folded(dot(stacked(u[i]), turn[i]), 48, PATCH) + a[i] * v[i] for i in todo]
            return [a[i] * t1[i] for i in todo], new

        def times_f1(a, u):
            a2, u2 = times_t1(a, u)
            return [1.5 * a[i] - 0.5 * a2[i] for i in todo], [1.5 * u[i] - 0.5 * u2[i] for i in todo]
        a, u = times_f1(a, u)
        a2, u2 = times_f1(*times_f1(*times_t1(a, u)))
        a = [1.5 * a[i] - 0.5 * a2[i] for i in todo]
        u = [1.5 * u[i] - 0.5 * u2[i] for i in todo]
        spread = [folded(dot(stacked(u[i]), patch[i]), 48, MEMBERS) for i in todo]
        for i, c in enumerate(cs):
            scale = jnp.sqrt(inv[i])
            scale = jnp.concatenate([scale, scale], axis=1)
            share = jnp.concatenate([a[i], a[i]], axis=1)
            moved = (share * pert[i] + spread[i][:ROWS]) * scale
            nudge = spread[i][ROWS:ROWS + 1] * scale
            out = moved + (mean[i] + jnp.sum(moved * nudge, axis=1, keepdims=True) * (1.0 / (MEMBERS - 1.0)))
            for m in range(2):
                for var in range(4):
                    analysed[pl.ds((m * 4 + var) * 16 + c, 8, stride=128), :] = out[var * 8:var * 8 + 8, m * 128:m * 128 + 128]
        return carry
    lax.fori_loop(0, COLS // BATCH, body, 0)


def turn_members(src, dst):
    for level in range(LEVELS):
        dst[pl.ds(level * 128, 128), :] = jnp.transpose(src[pl.ds(level, MEM, stride=8), :])


def turn_back(src, dst):
    for level in range(LEVELS):
        dst[pl.ds(level, MEM, stride=8), :] = jnp.transpose(src[pl.ds(level * 128, 128), :])


def kernel(state_in, branch_in, site_in, value_in, index_in, weight_in, result,
           state, branch, site, value, weight, stab, stab_edge, to_next, to_prev, from_prev, from_next, mixed, edge, tiles, columns, obs, table,
           index, fields, lookup, turned, gap, analysed, picked, steps, turns, norms, outgoing, landed, placed,
           halo_send, halo_recv, send_sems, plane_sems, x_sems, core_sem, out_sems, in_sems, load_sems, store_sems, arrived):
    me, tile = lax.axis_index("mem"), lax.axis_index("tile")
    greeting = greet(me, tile)
    next(greeting)
    loads = [pltpu.make_async_copy(state_in.at[:, m], state.at[:, pl.ds(m * 4, 4)], load_sems.at[m]) for m in range(2)]
    loads += [pltpu.make_async_copy(a, b, load_sems.at[2 + n]) for n, (a, b) in enumerate(
        ((branch_in, branch), (site_in, site), (value_in, value), (weight_in, weight),
         (index_in.at[0, pl.ds(pl.multiple_of(me * COLS, COLS), COLS)], index)))]
    for load in loads:
        load.start()

    def state_here():
        loads[0].wait()
        loads[1].wait()
    rounds = pass_on(arrived, me, tile)
    forecast_body(state, branch, stab, stab_edge, to_next, to_prev, from_prev, from_next, mixed, edge, halo_send, halo_recv, me, tile,
                  greeting, rounds, state_here, loads[2].wait)
    for load in loads[3:]:
        load.wait()
    slot = slot_of(me)
    here = pl.ds(pl.multiple_of(slot * 8, 8), 8)

    def send_columns():
        def to_owner(to):
            send(tiles.at[pl.ds(pl.multiple_of(to * 8, 8), 8)], columns.at[here], out_sems.at[0], in_sems.at[0], to, tile)
        each_device(me, to_owner)
        columns[here, :] = tiles[pl.ds(pl.multiple_of(me * 8, 8), 8), :]

    observe(mixed, site, obs)
    table[pl.ds(pl.multiple_of(slot * 16, 16), 16), :] = obs[...]
    gather = gather_obs(table, send_sems, plane_sems, x_sems, core_sem, me, tile)
    next(gather)
    cut_columns(mixed, tiles)
    for _ in rounds:
        pass
    if ORDER == 0:
        send_columns()
        next(gather)
    else:
        next(gather)
        send_columns()
    for _ in gather:
        pass
    prepare(table, value, index, weight, lookup, turned, gap)
    pick_obs(turned, lookup, picked)
    sweep(turned, weight, picked, steps, turns, norms)
    wait_rows(tiles, out_sems.at[0], 8 * (MEM - 1))
    wait_rows(columns, in_sems.at[0], 8 * (MEM - 1))
    turn_members(columns, fields)
    apply(fields, weight, gap, picked, steps, turns, norms, analysed)
    turn_back(analysed, outgoing)
    mine = pl.ds(pl.multiple_of(me * 8, 8), 8)

    def give_back(to):
        send(outgoing.at[pl.ds(pl.multiple_of(slot_of(to) * 8, 8), 8)], landed.at[mine], out_sems.at[1], in_sems.at[1], to, tile)
    each_device(me, give_back)
    landed[mine, :] = outgoing[here, :]
    wait_rows(outgoing, out_sems.at[1], 8 * (MEM - 1))
    wait_rows(landed, in_sems.at[1], 8 * (MEM - 1))
    place(landed, placed)
    whole = placed.reshape(4, ROWS, 8, LANES)
    stores = [pltpu.make_async_copy(whole.at[lt, :, pl.ds(m * 4, 4)], result.at[:, m, :, pl.ds(lt * LANES, LANES)], store_sems.at[lt * 2 + m])
              for lt in range(4) for m in range(2)]
    for store in stores:
        store.start()
    for store in stores:
        store.wait()


ORDER = 1


def place(landed, result):
    def body(n, carry):
        x, lt = div(n, 4), rem(n, 4)
        blocks = [landed[pl.ds(pl.multiple_of((x * 32 + lt * 8 + g) * 8, 8), 8), :] for g in range(8)]
        blocks = block_transpose(blocks)
        for m in range(2):
            for var in range(4):
                result[pl.ds(lt * 256 + var * 64 + m * 4 + x, 8, stride=8), :] = blocks[m * 4 + var]
        return carry
    lax.fori_loop(0, 16, body, 0, unroll=4)


def shape(*dims, dtype=F32):
    return jax.ShapeDtypeStruct(dims, dtype)


def per_device(state, branch, obs_site, obs_value, patch_index, patch_weight):
    dma = pltpu.SemaphoreType.DMA
    regular = pltpu.SemaphoreType.REGULAR

    def rows(n, width=LANES, dtype=F32):
        return pltpu.VMEM((n, width), dtype)
    result = pl.pallas_call(
        kernel,
        name="forecast_analysis",
        out_shape=shape(ROWS, 2, 4, WIDTH),
        in_specs=[HBM] * 6,
        out_specs=HBM,
        scratch_shapes=[
            pltpu.VMEM((ROWS, 8, WIDTH), F32), pltpu.VMEM((16, WIDTH), jnp.int32), rows(8, dtype=jnp.int32), rows(8), rows(COLS),
            rows(64), rows(64), rows(128, WIDTH), rows(128, WIDTH), rows(128, WIDTH), rows(128, WIDTH),
            rows(1024), rows(1024), rows(1024), rows(1024), rows(16), rows(MEM * 16),
            rows(COLS, LANES, jnp.int32), rows(1024), rows(OBS, 2 * MEMBERS, BF16), rows(LANES), rows(COLS), rows(1024),
            rows(COLS * PATCH, 2 * MEMBERS, BF16), rows(COLS * PATCH, 2 * PATCH, BF16), rows(COLS * PATCH, 2 * PATCH, BF16),
            rows(COLS), rows(1024), rows(1024), rows(1024),
            dma((2,)), dma((8,)), dma((3,)), dma((15,)), dma((3,)), dma(()), dma((2,)), dma((2,)), dma((7,)), dma((8,)), regular((3,)),
        ],
        compiler_params=pltpu.CompilerParams(collective_id=1, has_side_effects=True, vmem_limit_bytes=60 * 1024 * 1024),
    )(state.reshape(ROWS, 2, 4, WIDTH), branch, obs_site.reshape(8, LANES), obs_value.reshape(8, LANES), patch_index, patch_weight.reshape(COLS, LANES))
    return result.reshape(state.shape)


def solution(mesh):
    placed = (
        P(None, None, "mem", "tile", None),
        P(),
        P("tile", None),
        P("tile", None),
        P("tile", None, None),
        P("tile", "mem", None),
    )
    return jax.shard_map(
        per_device,
        mesh=mesh,
        in_specs=placed,
        out_specs=P(None, None, "mem", "tile", None),
        check_vma=False,
    )
```

```python
import jax
import jax.numpy as jnp
from jax import lax
from jax.experimental import pallas as pl
from jax.experimental.pallas import tpu as pltpu
from jax.sharding import PartitionSpec as P

MESH = pl.DeviceIdType.MESH
F32 = jnp.float32
BF16 = jnp.bfloat16
VMEM = pl.BlockSpec(memory_space=pltpu.VMEM)
HBM = pl.BlockSpec(memory_space=pltpu.HBM)
LEVELS, ROWS, WIDTH, LANES = 8, 32, 512, 128
MEM, COLS, MEMBERS, PATCH, OBS = 128, 16, 256, 128, 1024


def rem(a, b):
    return lax.rem(a, jnp.int32(b))


def div(a, b):
    return lax.div(a, jnp.int32(b))


def slot_of(device):
    core, y = rem(device, 2), rem(div(device, 2), 8)
    z, x = rem(div(device, 16), 2), div(device, 32)
    return core * 64 + x * 16 + y * 2 + z


def device_at(core, x, y, z):
    return x * 32 + z * 16 + y * 2 + core


def wait_rows(ref, sem, rows):
    part = ref.at[pl.ds(0, rows)]
    pltpu.make_async_copy(part, part, sem).wait()


def send(src, dst, send_sem, recv_sem, mem, tile):
    pltpu.make_async_remote_copy(
        src_ref=src, dst_ref=dst, send_sem=send_sem, recv_sem=recv_sem,
        device_id=(mem, tile), device_id_type=MESH,
    ).start()


def block_transpose(blocks):
    group = lax.broadcasted_iota(jnp.int32, (8, LANES), 1) // 16
    blocks = list(blocks)
    for bit in (1, 2, 4):
        upper = (group // bit) % 2 == 1
        for low in range(8):
            if low & bit:
                continue
            a, b = blocks[low], blocks[low + bit]
            blocks[low] = jnp.where(upper, pltpu.roll(b, 16 * bit, 1), a)
            blocks[low + bit] = jnp.where(upper, b, pltpu.roll(a, LANES - 16 * bit, 1))
    return blocks


def column_step(u, v, theta, energy, stab_m, stab_h):
    n = LEVELS
    km, kh, prod = [], [], []
    for k in range(n - 1):
        scale = 0.6 * jnp.sqrt(0.5 * (energy[k] + energy[k + 1]))
        km.append(scale * stab_m)
        kh.append(scale * stab_h)
        du, dv = u[k + 1] - u[k], v[k + 1] - v[k]
        prod.append(km[k] * (du * du + dv * dv))

    def solve(coef, extra, rhs):
        count = len(rhs)
        ratios, values = [], [[] for _ in range(count)]
        for k in range(n):
            pivot = 1.0 + extra[k] if extra is not None else 1.0
            if k > 0:
                pivot = pivot + coef[k - 1]
            if k < n - 1:
                pivot = pivot + coef[k]
            if k > 0:
                pivot = pivot - coef[k - 1] * ratios[-1]
            inverse = 1.0 / pivot
            for i in range(count):
                top = rhs[i][k]
                if k > 0:
                    top = top + coef[k - 1] * values[i][-1]
                values[i].append(top * inverse)
            if k < n - 1:
                ratios.append(coef[k] * inverse)
        out = []
        for i in range(count):
            result = [values[i][n - 1]]
            for k in range(n - 2, -1, -1):
                result.append(values[i][k] + ratios[k] * result[-1])
            out.append(result[::-1])
        return out

    source = []
    for k in range(n):
        if k == 0:
            total = prod[0]
        elif k == n - 1:
            total = prod[n - 2]
        else:
            total = prod[k - 1] + prod[k]
        source.append(energy[k] + 0.5 * total)
    sink = [0.3 * jnp.sqrt(energy[k]) for k in range(n)]
    new_u, new_v = solve(km, None, [u, v])
    (new_theta,) = solve(kh, None, [theta])
    (new_energy,) = solve(km, sink, [source])
    return new_u, new_v, new_theta, new_energy


def stabilities(branch):
    m = jnp.where(branch == 0, 0.25, jnp.where(branch == 1, 0.6, 1.2)).astype(F32)
    h = jnp.where(branch == 0, 0.15, jnp.where(branch == 1, 0.7, 1.6)).astype(F32)
    return m, h


def mix_columns(src, dst, stab_ref):
    def body(lt, carry):
        base = pl.multiple_of(lt * 256, 256)
        field = [[src[pl.ds(base + (var * 8 + k) * 8, 8), :] for k in range(LEVELS)] for var in range(4)]
        sbase = pl.multiple_of(lt * 16, 16)
        stab_m, stab_h = stab_ref[pl.ds(sbase, 8), :], stab_ref[pl.ds(sbase + 8, 8), :]
        new = column_step(*field, stab_m, stab_h)
        for var in range(4):
            for k in range(LEVELS):
                dst[pl.ds(base + (var * 8 + k) * 8, 8), :] = new[var][k]
        return carry
    lax.fori_loop(0, 4, body, 0)


def rows_of(ref, row):
    return jnp.broadcast_to(ref[pl.ds(row, 1), :], (8, WIDTH))


def laplace_step(centre, up, down):
    total = up + down + pltpu.roll(centre, 1, 1) + pltpu.roll(centre, WIDTH - 1, 1) - 4.0 * centre
    return centre + 0.2 * total


def put_tiles(dst, row, value):
    for lt in range(4):
        dst[pl.ds(pl.multiple_of(lt * 256 + row * 8, 8), 8), :] = value[:, lt * LANES:(lt + 1) * LANES]


def get_tiles(src, row):
    return jnp.concatenate(
        [src[pl.ds(pl.multiple_of(lt * 256 + row * 8, 8), 8), :] for lt in range(4)], axis=1)


def forecast_body(state, branch, stab, stab_edge, to_next, to_prev, from_prev, from_next, mixed, edge, halo_send, halo_recv, me, tile, greeting, rounds, state_here, branch_here, meanwhile):
    sub = lax.broadcasted_iota(jnp.int32, (8, WIDTH), 0)
    next_tile, prev_tile = rem(tile + 1, 4), rem(tile + 3, 4)
    state_here()

    def pack(row, carry):
        for q, (n_sub, p_sub) in enumerate(((3, 0), (7, 4), (2, 1), (6, 5))):
            to_next[pl.ds(row * 4 + q, 1), :] = state[row, pl.ds(n_sub, 1), :]
            to_prev[pl.ds(row * 4 + q, 1), :] = state[row, pl.ds(p_sub, 1), :]
        return carry
    lax.fori_loop(0, ROWS, pack, 0, unroll=4)
    for _ in greeting:
        pass
    for var in range(4):
        rows = pl.ds(var * 32, 32)
        send(to_next.at[rows], from_prev.at[rows], halo_send.at[0], halo_recv.at[var], me, next_tile)
        send(to_prev.at[rows], from_next.at[rows], halo_send.at[1], halo_recv.at[4 + var], me, prev_tile)
    next(rounds)

    branch_here()
    own = [rows_of(branch, tile * 4 + x) for x in range(4)]
    before, after = rows_of(branch, rem(tile * 4 + 15, 16)), rows_of(branch, rem(tile * 4 + 4, 16))
    x_of = sub % 4
    own_rows = jnp.where(x_of == 0, own[0], jnp.where(x_of == 1, own[1], jnp.where(x_of == 2, own[2], own[3])))
    edge_rows = jnp.where(x_of < 2, before, after)
    for ref, rows in ((stab, own_rows), (stab_edge, edge_rows)):
        m, h = stabilities(rows)
        for lt in range(4):
            ref[pl.ds(lt * 16, 8), :] = m[:, lt * LANES:(lt + 1) * LANES]
            ref[pl.ds(lt * 16 + 8, 8), :] = h[:, lt * LANES:(lt + 1) * LANES]
    next(rounds)
    meanwhile()

    def pick(a, b, c, d):
        return jnp.where(x_of == 0, a, jnp.where(x_of == 1, b, jnp.where(x_of == 2, c, d)))

    def first(row, carry):
        centre = state[row]
        left = [rows_of(from_prev, row * 4 + q) for q in range(4)]
        right = [rows_of(from_next, row * 4 + q) for q in range(4)]
        up = jnp.where(x_of == 0, jnp.where(sub < 4, left[0], left[1]), pltpu.roll(centre, 1, 0))
        down = jnp.where(x_of == 3, jnp.where(sub < 4, right[0], right[1]), pltpu.roll(centre, 7, 0))
        put_tiles(mixed, row, laplace_step(centre, up, down))
        inner = [jnp.broadcast_to(state[row, pl.ds(s, 1), :], (8, WIDTH)) for s in (0, 4, 3, 7)]
        edge_centre = pick(left[0], left[1], right[0], right[1])
        outer = pick(left[2], left[3], right[2], right[3])
        put_tiles(edge, row, laplace_step(edge_centre, outer, pick(*inner)))
        return carry
    for var in range(4):
        wait_rows(from_prev, halo_recv.at[var], 32)
        wait_rows(from_next, halo_recv.at[4 + var], 32)
        lax.fori_loop(var * 8, var * 8 + 8, first, 0, unroll=8)
    mix_columns(mixed, mixed, stab)
    mix_columns(edge, edge, stab_edge)
    next(rounds)

    def second(row, carry):
        centre = get_tiles(mixed, row)
        sides = get_tiles(edge, row)
        side = [jnp.broadcast_to(sides[q:q + 1, :], (8, WIDTH)) for q in range(4)]
        up = jnp.where(x_of == 0, jnp.where(sub < 4, side[0], side[1]), pltpu.roll(centre, 1, 0))
        down = jnp.where(x_of == 3, jnp.where(sub < 4, side[2], side[3]), pltpu.roll(centre, 7, 0))
        put_tiles(mixed, row, laplace_step(centre, up, down))
        return carry
    lax.fori_loop(0, ROWS, second, 0, unroll=8)
    mix_columns(mixed, mixed, stab)
    wait_rows(to_next, halo_send.at[0], 128)
    wait_rows(to_prev, halo_send.at[1], 128)


def mark_sites(site, sites_at):
    columns = site[...] % 2048

    def body(n, carry):
        rows = pl.ds(pl.multiple_of(n * 256, 256), 256)
        place = lax.broadcasted_iota(jnp.int32, (256, LANES), 0) + n * 256
        for b in range(8):
            sites_at[rows, pl.ds(b * LANES, LANES)] = (place == columns[b:b + 1, :]).astype(F32).astype(BF16)
        return carry
    lax.fori_loop(0, 8, body, 0)


def mark_patch(index, weight, turned, chosen):
    turned[...] = jnp.transpose(jnp.concatenate([index[...].astype(F32), weight[...], jnp.zeros((96, LANES), F32)], axis=0))
    places = lax.broadcasted_iota(jnp.int32, (PATCH, OBS), 1)

    def body(n, carry):
        here = pltpu.roll(turned[...], LANES - n * 2, 1)
        for i in range(2):
            rows = pl.ds(pl.multiple_of((n * 2 + i) * PATCH, PATCH), PATCH)
            chosen[rows, :] = (places == here[:, i:i + 1].astype(jnp.int32)).astype(F32).astype(BF16)
        return carry
    lax.fori_loop(0, COLS // 2, body, 0)


def observe(mixed, site, sites_at, parts, obs):
    def body(n, carry):
        x, lt = div(n, 4), rem(n, 4)
        left = jnp.concatenate([mixed[pl.ds(lt * 256 + var * 64 + m * 4 + x, 8, stride=8), :] for m in range(2) for var in range(4)], axis=0)
        for part in range(3):
            piece = left.astype(BF16)
            parts[pl.ds(part * 64, 64), pl.ds(pl.multiple_of(n * LANES, LANES), LANES)] = piece
            left = left - piece.astype(F32)
        return carry
    lax.fori_loop(0, 16, body, 0, unroll=4)
    row = lax.broadcasted_iota(jnp.int32, (ROWS, LANES), 0)
    wanted = site[...] // 2048
    for b in range(0, 8, 2):
        found = dot(parts[...], sites_at[:, b * LANES:(b + 2) * LANES])
        found = found[:64] + (found[64:128] + found[128:])
        for i in range(2):
            for m in range(2):
                one = jnp.where(row == wanted[b + i:b + i + 1, :], found[m * ROWS:(m + 1) * ROWS, i * LANES:(i + 1) * LANES], 0.0)
                obs[pl.ds(m * 8 + b + i, 1), :] = jnp.sum(one, axis=0, keepdims=True)


def cut_columns(mixed, tiles):
    def body(n, carry):
        x, lt = div(n, 4), rem(n, 4)
        blocks = [mixed[pl.ds(lt * 256 + var * 64 + m * 4 + x, 8, stride=8), :] for m in range(2) for var in range(4)]
        for g, block in enumerate(block_transpose(blocks)):
            tiles[pl.ds(pl.multiple_of((x * 32 + lt * 8 + g) * 8, 8), 8), :] = block
        return carry
    lax.fori_loop(0, 16, body, 0, unroll=4)


def gather_obs(table, send_sems, plane_sems, x_sems, core_sem, me, tile):
    core, y, z, x = rem(me, 2), rem(div(me, 2), 8), rem(div(me, 16), 2), div(me, 32)

    def part(first, count):
        return table.at[pl.ds(pl.multiple_of(first * 16, count * 16), count * 16)]

    def slot(y_of, z_of):
        return part(core * 64 + x * 16 + y_of * 2 + z_of, 1)

    def pass_slot(one):
        for j in (2, 1, 3):
            send(one, one, send_sems.at[1], x_sems.at[j - 1], device_at(core, rem(x + j, 4), y, z), tile)
        send(one, one, send_sems.at[2], core_sem, device_at(1 - core, x, y, z), tile)
    own = slot(y, z)
    for i in (4, 3, 5, 2, 6, 1, 7, 0):
        send(own, own, send_sems.at[0], plane_sems.at[7 + i], device_at(core, x, rem(y + i, 8), 1 - z), tile)
        if i:
            send(own, own, send_sems.at[0], plane_sems.at[i - 1], device_at(core, x, rem(y + i, 8), z), tile)
    pass_slot(own)
    yield
    for i in (1, 7, 2, 6, 3, 5, 4):
        wait_rows(table, plane_sems.at[i - 1], 16)
        pass_slot(slot(rem(y + 8 - i, 8), z))
    for i in (0, 1, 7, 2, 6, 3, 5, 4):
        wait_rows(table, plane_sems.at[7 + i], 16)
        pass_slot(slot(rem(y + 8 - i, 8), 1 - z))
    yield
    for j in (1, 3, 2):
        wait_rows(table, x_sems.at[j - 1], 256)
        plane = part(core * 64 + rem(x + 4 - j, 4) * 16, 16)
        send(plane, plane, send_sems.at[2], core_sem, device_at(1 - core, x, y, z), tile)
    wait_rows(table, core_sem, 1024)
    wait_rows(table, send_sems.at[0], 16 * 15)
    wait_rows(table, send_sems.at[1], 256 * 3)
    wait_rows(table, send_sems.at[2], 1024)


def each_device(me, do):
    core, y, z, x = rem(me, 2), rem(div(me, 2), 8), rem(div(me, 16), 2), div(me, 32)

    def all_at(y_to, z_to, own):
        for i in (2, 1, 3, 0):
            for c in (1, 0):
                if not (own and i == 0 and c == 0):
                    do(device_at(rem(core + c, 2), rem(x + i, 4), y_to, z_to))

    def body(z_to):
        def one(n, carry):
            half = div(n + 1, 2)
            step = rem(12 + (2 * rem(n, 2) - 1) * half, 8)
            all_at(rem(y + step, 8), z_to, False)
            return carry
        return one
    lax.fori_loop(0, 8, body(1 - z), 0)
    lax.fori_loop(0, 7, body(z), 0)
    all_at(y, z, True)


def near(me):
    core, y, z, x = rem(me, 2), rem(div(me, 2), 8), rem(div(me, 16), 2), div(me, 32)
    return (
        [device_at(core, x, rem(y + i, 8), z) for i in range(1, 8)] + [device_at(core, x, rem(y + i, 8), 1 - z) for i in range(8)],
        [device_at(core, rem(x + i, 4), y, z) for i in range(1, 4)],
        [device_at(1 - core, x, y, z)],
    )


def greet(me, tile):
    barrier = pltpu.get_barrier_semaphore()
    for step in (1, 3):
        pl.semaphore_signal(barrier, inc=1, device_id=(me, rem(tile + step, 4)), device_id_type=MESH)
    for group in near(me):
        for to in group:
            pl.semaphore_signal(barrier, inc=1, device_id=(to, tile), device_id_type=MESH)
    yield
    pl.semaphore_wait(barrier, 2 + 15 + 3 + 1)


def pass_on(arrived, me, tile):
    for n, group in enumerate(near(me)):
        for to in group:
            pl.semaphore_signal(arrived.at[n], inc=1, device_id=(to, tile), device_id_type=MESH)
        yield
        pl.semaphore_wait(arrived.at[n], len(group))


def split(a):
    high = a.astype(BF16)
    return high, (a - high.astype(F32)).astype(BF16)


def dot(a, b):
    return jnp.dot(a, b, preferred_element_type=F32)


def dot_t(a, b):
    return lax.dot_general(a, b, (((1,), (1,)), ((), ())), preferred_element_type=F32)


def dot3(a, pair):
    high, low = split(a)
    return dot(high, pair[0]) + (dot(low, pair[0]) + dot(high, pair[1]))


def prepare(table, value, index, lookup, gap):
    total = table[pl.ds(0, 16), :]
    total = lax.fori_loop(1, MEM, lambda s, t: t + table[pl.ds(pl.multiple_of(s * 16, 16), 16), :], total)
    mean = (total[:8] + total[8:]) * (1.0 / MEMBERS)
    diff = value[...] - mean
    for b in range(8):
        for m in range(2):
            block = table[pl.ds(m * 8 + b, MEM, stride=16), :] - mean[b:b + 1, :]
            high, low = split(jnp.transpose(block))
            lookup[pl.ds(b * 128, 128), pl.ds(m * 128, 128)] = high
            lookup[pl.ds(b * 128, 128), pl.ds(256 + m * 128, 128)] = low
    indices = index[...]
    for part in range(2):
        own = indices[part * 8:part * 8 + 8]
        found = jnp.zeros((8, LANES), F32)
        for b in range(8):
            row = jnp.broadcast_to(diff[b:b + 1, :], (8, LANES))
            taken = jnp.take_along_axis(row, own % 128, axis=1, mode="promise_in_bounds")
            found = jnp.where(own // 128 == b, taken, found)
        gap[pl.ds(part * 8, 8), :] = found


def eye():
    shape = (PATCH, PATCH)
    return (lax.broadcasted_iota(jnp.int32, shape, 0) == lax.broadcasted_iota(jnp.int32, shape, 1)).astype(F32)


def stacked(a):
    return jnp.concatenate(split(a), axis=0)


def beside(a):
    return jnp.concatenate(split(a), axis=1)


def folded(p, rows, width):
    return (p[:rows, :width] + p[rows:, :width]) + (p[:rows, width:] + p[rows:, width:])


def pick_obs(chosen, lookup, picked):
    for n in range(2):
        rows = pl.ds(n * 1024, 1024)
        picked[rows, :] = dot(chosen[rows, :], lookup[...]).astype(BF16)


def patch_of(picked, c):
    return picked[pl.ds(pl.multiple_of(c * PATCH, PATCH), PATCH), :]


def sweep(turned, weight, gap, picked, turns, norms, shares, nudges):
    columns = range(COLS)
    one = eye()

    def c_rate(t):
        return 2.25 - 1.5 * t + 0.25 * t * t

    def h(t, y, square):
        return c_rate(t) * one + (0.25 * t - 1.5) * y + 0.25 * square

    def times(a, wide):
        return [folded(dot(stacked(m), k), m.shape[0], PATCH) for m, k in zip(a, wide)]
    patch = [patch_of(picked, c) for c in columns]
    both = [jnp.concatenate([p[:, :MEMBERS], p[:, MEMBERS:]], axis=0) for p in patch]
    cov = [folded(dot_t(q, q), PATCH, PATCH) for q in both]
    cov_w = [v * (weight[pl.ds(c, 1), :] * (1.0 / (MEMBERS - 1.0))) for v, c in zip(cov, columns)]
    t = []
    for c in columns:
        column = turned[:, COLS + c:COLS + c + 1] * (1.0 / (MEMBERS - 1.0))
        total = jnp.sum(cov_w[c] * (2.0 * one + cov[c] * column), axis=0, keepdims=True)
        total = jnp.sum(total, axis=1, keepdims=True)
        t.append(jnp.broadcast_to(1.0 / jnp.sqrt(MEMBERS + total), (1, PATCH)))
    k = [(one + v) * r for v, r in zip(cov_w, t)]
    k_wide = [beside(m) for m in k]
    k_square = times(k, k_wide)
    h_k = [h(r, m, q) for r, m, q in zip(t, k, k_square)]
    turn = times([2.25 * one - 1.5 * m + 0.25 * q for m, q in zip(k, k_square)], k_wide)
    t1 = [r * c_rate(r) for r in t]
    turn_wide = [beside(m) for m in turn]
    turn_square = times(turn, turn_wide)
    second = times([2.25 * one - 1.5 * m + 0.25 * q for m, q in zip(turn, turn_square)], turn_wide)
    f0, f1 = [1.5 - 0.5 * r for r in t], [1.5 - 0.5 * r for r in t1]
    f2 = [1.5 - 0.5 * r * c_rate(r) for r in t1]
    left = times([1.5 * one - 0.5 * m + a * b for m, a, b in zip(turn, f0, h_k)], [beside(1.5 * one - 0.5 * m) for m in second])
    right = times([a * b * m for a, b, m in zip(f0, f1, h_k)], [beside(h(r, m, q)) for r, m, q in zip(t1, turn, turn_square)])
    wide = [beside(-0.5 * (a + b)) for a, b in zip(left, right)]
    first_row = lax.broadcasted_iota(jnp.int32, (16, PATCH), 0) == 0
    force = [jnp.where(first_row, weight[pl.ds(c, 1), :] * gap[pl.ds(c, 1), :], 0.0) for c in columns]
    share = [a * b * c for a, b, c in zip(f0, f1, f2)]
    ahead = [m - r * a for m, r, a in zip(times(force, k_wide), t, force)]
    force = [a * b + m for a, b, m in zip(share, force, times(ahead, wide))]
    for c in columns:
        turns[pl.ds(c * PATCH, PATCH), :] = wide[c]
        norms[pl.ds(c, 1), :] = t[c]
        shares[pl.ds(c, 1), :] = share[c]
        scale = jnp.sqrt(t[c])
        nudges[pl.ds(c, 1), :] = folded(dot(stacked(force[c]), patch[c]), 16, MEMBERS)[:1] * jnp.concatenate([scale, scale], axis=1)


def apply(fields, weight, picked, turns, norms, shares, nudges, analysed):
    columns = range(COLS)
    x = []
    for c in columns:
        parts = [fields[pl.ds((m * 4 + var) * 16 + c, 8, stride=128), :] for m in range(2) for var in range(4)]
        x.append(jnp.concatenate([jnp.concatenate(parts[:4], axis=0), jnp.concatenate(parts[4:], axis=0)], axis=1))
    mean = [jnp.sum(a, axis=1, keepdims=True) * (1.0 / MEMBERS) for a in x]
    pert = [a - b for a, b in zip(x, mean)]
    patch = [patch_of(picked, c) for c in columns]
    cross = []
    for c in columns:
        p = jnp.concatenate([patch[c][:, :MEMBERS], patch[c][:, MEMBERS:]], axis=0)
        scale = weight[pl.ds(c, 1), :] * norms[pl.ds(c, 1), :] * (1.0 / (MEMBERS - 1.0))
        cross.append(folded(dot_t(stacked(pert[c]), p), ROWS, PATCH) * scale)
    u = [folded(dot(stacked(cross[c]), patch_of(turns, c)), ROWS, PATCH) for c in columns]
    spread = [folded(dot(stacked(u[c]), patch[c]), ROWS, MEMBERS) for c in columns]
    for c in columns:
        scale, share = jnp.sqrt(norms[pl.ds(c, 1), :]), shares[pl.ds(c, 1), :]
        scale, share = jnp.concatenate([scale, scale], axis=1), jnp.concatenate([share, share], axis=1)
        moved = (share * pert[c] + spread[c]) * scale
        out = moved + (mean[c] + jnp.sum(moved * nudges[pl.ds(c, 1), :], axis=1, keepdims=True) * (1.0 / (MEMBERS - 1.0)))
        for m in range(2):
            for var in range(4):
                analysed[pl.ds((m * 4 + var) * 16 + c, 8, stride=128), :] = out[var * 8:var * 8 + 8, m * 128:m * 128 + 128]


def turn_members(src, dst):
    for level in range(LEVELS):
        dst[pl.ds(level * 128, 128), :] = jnp.transpose(src[pl.ds(level, MEM, stride=8), :])


def turn_back(src, dst):
    for level in range(LEVELS):
        dst[pl.ds(level, MEM, stride=8), :] = jnp.transpose(src[pl.ds(level * 128, 128), :])


def kernel(state_in, branch_in, site_in, value_in, index_in, weight_in, result,
           state, branch, site, value, weight, stab, stab_edge, to_next, to_prev, from_prev, from_next, mixed, edge, tiles, columns, obs, table,
           index, fields, lookup, turned, gap, analysed, picked, shares, turns, norms, nudges, outgoing, landed, placed, sites_at, parts, chosen,
           halo_send, halo_recv, send_sems, plane_sems, x_sems, core_sem, out_sems, in_sems, back_sems, load_sems, store_sems, arrived):
    me, tile = lax.axis_index("mem"), lax.axis_index("tile")
    greeting = greet(me, tile)
    next(greeting)
    loads = [pltpu.make_async_copy(state_in.at[:, m], state.at[:, pl.ds(m * 4, 4)], load_sems.at[m]) for m in range(2)]
    loads += [pltpu.make_async_copy(a, b, load_sems.at[2 + n]) for n, (a, b) in enumerate(
        ((branch_in, branch), (site_in, site), (value_in, value), (weight_in, weight),
         (index_in.at[0, pl.ds(pl.multiple_of(me * COLS, COLS), COLS)], index)))]
    for load in loads:
        load.start()

    def state_here():
        loads[0].wait()
        loads[1].wait()

    def meanwhile():
        for load in loads[3:]:
            load.wait()
        mark_sites(site, sites_at)
        mark_patch(index, weight, turned, chosen)
    rounds = pass_on(arrived, me, tile)
    forecast_body(state, branch, stab, stab_edge, to_next, to_prev, from_prev, from_next, mixed, edge, halo_send, halo_recv, me, tile,
                  greeting, rounds, state_here, loads[2].wait, meanwhile)
    slot = slot_of(me)
    here = pl.ds(pl.multiple_of(slot * 8, 8), 8)

    def to_owner(to):
        send(tiles.at[pl.ds(pl.multiple_of(to * 8, 8), 8)], columns.at[here], out_sems.at[0], in_sems.at[0], to, tile)
    observe(mixed, site, sites_at, parts, obs)
    table[pl.ds(pl.multiple_of(slot * 16, 16), 16), :] = obs[...]
    gather = gather_obs(table, send_sems, plane_sems, x_sems, core_sem, me, tile)
    next(gather)
    cut_columns(mixed, tiles)
    for _ in rounds:
        pass
    next(gather)
    each_device(me, to_owner)
    columns[here, :] = tiles[pl.ds(pl.multiple_of(me * 8, 8), 8), :]
    for _ in gather:
        pass
    prepare(table, value, index, lookup, gap)
    pick_obs(chosen, lookup, picked)
    sweep(turned, weight, gap, picked, turns, norms, shares, nudges)
    wait_rows(tiles, out_sems.at[0], 8 * (MEM - 1))
    wait_rows(columns, in_sems.at[0], 8 * (MEM - 1))
    turn_members(columns, fields)
    apply(fields, weight, picked, turns, norms, shares, nudges, analysed)
    turn_back(analysed, outgoing)
    mine = pl.ds(pl.multiple_of(me * 8, 8), 8)

    def give_back(to):
        send(outgoing.at[pl.ds(pl.multiple_of(slot_of(to) * 8, 8), 8)], landed.at[mine], out_sems.at[1], back_sems.at[div(me, 8)], to, tile)
    each_device(me, give_back)
    pltpu.make_async_copy(outgoing.at[here], landed.at[mine], back_sems.at[div(me, 8)]).start()
    whole = placed.reshape(4, ROWS, 8, LANES)
    stores = []
    for i in range(1, 5):
        lt = rem(div(me, 8) + i, 4)
        for x in range(4):
            wait_rows(landed, back_sems.at[x * 4 + lt], 64)
        for x in range(4):
            place(landed, placed, x, lt)
        for m in range(2):
            lanes = pl.ds(pl.multiple_of(lt * LANES, LANES), LANES)
            stores.append(pltpu.make_async_copy(whole.at[lt, :, pl.ds(m * 4, 4)], result.at[:, m, :, lanes], store_sems.at[i * 2 - 2 + m]))
            stores[-1].start()
    wait_rows(outgoing, out_sems.at[1], 8 * (MEM - 1))
    for store in stores:
        store.wait()


def copy_kernel(source, result, held, sems):
    parts = [pl.ds(n * 8, 8) for n in range(4)]
    reads = [pltpu.make_async_copy(source.at[p], held.at[p], sems.at[n]) for n, p in enumerate(parts)]
    writes = [pltpu.make_async_copy(held.at[p], result.at[p], sems.at[4 + n]) for n, p in enumerate(parts)]
    for read in reads:
        read.start()
    for read, write in zip(reads, writes):
        read.wait()
        write.start()
    for write in writes:
        write.wait()


def place(landed, result, x, lt):
    blocks = [landed[pl.ds(pl.multiple_of((x * 32 + lt * 8 + g) * 8, 8), 8), :] for g in range(8)]
    blocks = block_transpose(blocks)
    for m in range(2):
        for var in range(4):
            result[pl.ds(lt * 256 + var * 64 + m * 4 + x, 8, stride=8), :] = blocks[m * 4 + var]


def shape(*dims, dtype=F32):
    return jax.ShapeDtypeStruct(dims, dtype)


def per_device(state, branch, obs_site, obs_value, patch_index, patch_weight):
    dma = pltpu.SemaphoreType.DMA
    regular = pltpu.SemaphoreType.REGULAR

    def rows(n, width=LANES, dtype=F32):
        return pltpu.VMEM((n, width), dtype)
    result = pl.pallas_call(
        kernel,
        name="forecast_analysis",
        out_shape=shape(ROWS, 2, 4, WIDTH),
        in_specs=[HBM] * 6,
        out_specs=HBM,
        scratch_shapes=[
            pltpu.VMEM((ROWS, 8, WIDTH), F32), pltpu.VMEM((16, WIDTH), jnp.int32), rows(8, dtype=jnp.int32), rows(8), rows(COLS),
            rows(64), rows(64), rows(128, WIDTH), rows(128, WIDTH), rows(128, WIDTH), rows(128, WIDTH),
            rows(1024), rows(1024), rows(1024), rows(1024), rows(16), rows(MEM * 16),
            rows(COLS, LANES, jnp.int32), rows(1024), rows(OBS, 2 * MEMBERS, BF16), rows(LANES), rows(COLS), rows(1024),
            rows(COLS * PATCH, 2 * MEMBERS, BF16), rows(COLS), rows(COLS * PATCH, 2 * PATCH, BF16),
            rows(COLS), rows(COLS, MEMBERS), rows(1024), rows(1024), rows(1024),
            rows(2048, OBS, BF16), rows(192, 2048, BF16), rows(COLS * PATCH, OBS, BF16),
            dma((2,)), dma((8,)), dma((3,)), dma((15,)), dma((3,)), dma(()), dma((2,)), dma((1,)), dma((16,)), dma((7,)), dma((8,)), regular((3,)),
        ],
        compiler_params=pltpu.CompilerParams(collective_id=1, has_side_effects=True, vmem_limit_bytes=60 * 1024 * 1024),
    )(state.reshape(ROWS, 2, 4, WIDTH), branch, obs_site.reshape(8, LANES), obs_value.reshape(8, LANES), patch_index, patch_weight.reshape(COLS, LANES))
    result = pl.pallas_call(
        copy_kernel,
        name="copy_out",
        out_shape=shape(ROWS, 2, 4, WIDTH),
        in_specs=[HBM],
        out_specs=HBM,
        scratch_shapes=[pltpu.VMEM((ROWS, 2, 4, WIDTH), F32), dma((8,))],
        compiler_params=pltpu.CompilerParams(vmem_limit_bytes=60 * 1024 * 1024),
    )(result)
    return result.reshape(state.shape)


def solution(mesh):
    placed = (
        P(None, None, "mem", "tile", None),
        P(),
        P("tile", None),
        P("tile", None),
        P("tile", None, None),
        P("tile", "mem", None),
    )
    return jax.shard_map(
        per_device,
        mesh=mesh,
        in_specs=placed,
        out_specs=P(None, None, "mem", "tile", None),
        check_vma=False,
    )
```

```python
import jax
import jax.numpy as jnp
from jax import lax
from jax.experimental import pallas as pl
from jax.experimental.pallas import tpu as pltpu
from jax.sharding import PartitionSpec as P

MESH = pl.DeviceIdType.MESH
F32 = jnp.float32
BF16 = jnp.bfloat16
VMEM = pl.BlockSpec(memory_space=pltpu.VMEM)
HBM = pl.BlockSpec(memory_space=pltpu.HBM)
LEVELS, ROWS, WIDTH, LANES = 8, 32, 512, 128
MEM, COLS, MEMBERS, PATCH, OBS = 128, 16, 256, 128, 1024


def rem(a, b):
    return lax.rem(a, jnp.int32(b))


def div(a, b):
    return lax.div(a, jnp.int32(b))


def slot_of(device):
    core, y = rem(device, 2), rem(div(device, 2), 8)
    z, x = rem(div(device, 16), 2), div(device, 32)
    return core * 64 + x * 16 + y * 2 + z


def device_at(core, x, y, z):
    return x * 32 + z * 16 + y * 2 + core


def wait_rows(ref, sem, rows):
    part = ref.at[pl.ds(0, rows)]
    pltpu.make_async_copy(part, part, sem).wait()


def send(src, dst, send_sem, recv_sem, mem, tile):
    pltpu.make_async_remote_copy(
        src_ref=src, dst_ref=dst, send_sem=send_sem, recv_sem=recv_sem,
        device_id=(mem, tile), device_id_type=MESH,
    ).start()


def block_transpose(blocks):
    group = lax.broadcasted_iota(jnp.int32, (8, LANES), 1) // 16
    blocks = list(blocks)
    for bit in (1, 2, 4):
        upper = (group // bit) % 2 == 1
        for low in range(8):
            if low & bit:
                continue
            a, b = blocks[low], blocks[low + bit]
            blocks[low] = jnp.where(upper, pltpu.roll(b, 16 * bit, 1), a)
            blocks[low + bit] = jnp.where(upper, b, pltpu.roll(a, LANES - 16 * bit, 1))
    return blocks


def column_step(u, v, theta, energy, stab_m, stab_h):
    n = LEVELS
    km, kh, prod = [], [], []
    for k in range(n - 1):
        scale = 0.6 * jnp.sqrt(0.5 * (energy[k] + energy[k + 1]))
        km.append(scale * stab_m)
        kh.append(scale * stab_h)
        du, dv = u[k + 1] - u[k], v[k + 1] - v[k]
        prod.append(km[k] * (du * du + dv * dv))

    def solve(coef, extra, rhs):
        count = len(rhs)
        ratios, values = [], [[] for _ in range(count)]
        for k in range(n):
            pivot = 1.0 + extra[k] if extra is not None else 1.0
            if k > 0:
                pivot = pivot + coef[k - 1]
            if k < n - 1:
                pivot = pivot + coef[k]
            if k > 0:
                pivot = pivot - coef[k - 1] * ratios[-1]
            inverse = 1.0 / pivot
            for i in range(count):
                top = rhs[i][k]
                if k > 0:
                    top = top + coef[k - 1] * values[i][-1]
                values[i].append(top * inverse)
            if k < n - 1:
                ratios.append(coef[k] * inverse)
        out = []
        for i in range(count):
            result = [values[i][n - 1]]
            for k in range(n - 2, -1, -1):
                result.append(values[i][k] + ratios[k] * result[-1])
            out.append(result[::-1])
        return out

    source = []
    for k in range(n):
        if k == 0:
            total = prod[0]
        elif k == n - 1:
            total = prod[n - 2]
        else:
            total = prod[k - 1] + prod[k]
        source.append(energy[k] + 0.5 * total)
    sink = [0.3 * jnp.sqrt(energy[k]) for k in range(n)]
    new_u, new_v = solve(km, None, [u, v])
    (new_theta,) = solve(kh, None, [theta])
    (new_energy,) = solve(km, sink, [source])
    return new_u, new_v, new_theta, new_energy


def stabilities(branch):
    m = jnp.where(branch == 0, 0.25, jnp.where(branch == 1, 0.6, 1.2)).astype(F32)
    h = jnp.where(branch == 0, 0.15, jnp.where(branch == 1, 0.7, 1.6)).astype(F32)
    return m, h


def mix_columns(*sets):
    def body(lt, carry):
        base, sbase = pl.multiple_of(lt * 256, 256), pl.multiple_of(lt * 16, 16)
        new = []
        for ref, stab in sets:
            field = [[ref[pl.ds(base + (var * 8 + k) * 8, 8), :] for k in range(LEVELS)] for var in range(4)]
            new.append(column_step(*field, stab[pl.ds(sbase, 8), :], stab[pl.ds(sbase + 8, 8), :]))
        for (ref, stab), values in zip(sets, new):
            for var in range(4):
                for k in range(LEVELS):
                    ref[pl.ds(base + (var * 8 + k) * 8, 8), :] = values[var][k]
        return carry
    lax.fori_loop(0, 4, body, 0)


def rows_of(ref, row):
    return jnp.broadcast_to(ref[pl.ds(row, 1), :], (8, WIDTH))


def laplace_step(centre, up, down):
    total = up + down + pltpu.roll(centre, 1, 1) + pltpu.roll(centre, WIDTH - 1, 1) - 4.0 * centre
    return centre + 0.2 * total


def put_tiles(dst, row, value):
    for lt in range(4):
        dst[pl.ds(pl.multiple_of(lt * 256 + row * 8, 8), 8), :] = value[:, lt * LANES:(lt + 1) * LANES]


def get_tiles(src, row):
    return jnp.concatenate(
        [src[pl.ds(pl.multiple_of(lt * 256 + row * 8, 8), 8), :] for lt in range(4)], axis=1)


def forecast_body(state, branch, stab, stab_edge, to_next, to_prev, from_prev, from_next, mixed, edge, halo_send, halo_recv, me, tile, greeting, rounds, state_here, branch_here, meanwhile):
    sub = lax.broadcasted_iota(jnp.int32, (8, WIDTH), 0)
    next_tile, prev_tile = rem(tile + 1, 4), rem(tile + 3, 4)
    state_here()

    def pack(row, carry):
        for q, (n_sub, p_sub) in enumerate(((3, 0), (7, 4), (2, 1), (6, 5))):
            to_next[pl.ds(row * 4 + q, 1), :] = state[row, pl.ds(n_sub, 1), :]
            to_prev[pl.ds(row * 4 + q, 1), :] = state[row, pl.ds(p_sub, 1), :]
        return carry
    lax.fori_loop(0, ROWS, pack, 0, unroll=4)
    for _ in greeting:
        pass
    for var in range(4):
        rows = pl.ds(var * 32, 32)
        send(to_next.at[rows], from_prev.at[rows], halo_send.at[0], halo_recv.at[var], me, next_tile)
        send(to_prev.at[rows], from_next.at[rows], halo_send.at[1], halo_recv.at[4 + var], me, prev_tile)
    next(rounds)

    branch_here()
    own = [rows_of(branch, tile * 4 + x) for x in range(4)]
    before, after = rows_of(branch, rem(tile * 4 + 15, 16)), rows_of(branch, rem(tile * 4 + 4, 16))
    x_of = sub % 4
    own_rows = jnp.where(x_of == 0, own[0], jnp.where(x_of == 1, own[1], jnp.where(x_of == 2, own[2], own[3])))
    edge_rows = jnp.where(x_of < 2, before, after)
    for ref, rows in ((stab, own_rows), (stab_edge, edge_rows)):
        m, h = stabilities(rows)
        for lt in range(4):
            ref[pl.ds(lt * 16, 8), :] = m[:, lt * LANES:(lt + 1) * LANES]
            ref[pl.ds(lt * 16 + 8, 8), :] = h[:, lt * LANES:(lt + 1) * LANES]
    next(rounds)
    meanwhile()

    def pick(a, b, c, d):
        return jnp.where(x_of == 0, a, jnp.where(x_of == 1, b, jnp.where(x_of == 2, c, d)))

    def first(row, carry):
        centre = state[row]
        left = [rows_of(from_prev, row * 4 + q) for q in range(4)]
        right = [rows_of(from_next, row * 4 + q) for q in range(4)]
        up = jnp.where(x_of == 0, jnp.where(sub < 4, left[0], left[1]), pltpu.roll(centre, 1, 0))
        down = jnp.where(x_of == 3, jnp.where(sub < 4, right[0], right[1]), pltpu.roll(centre, 7, 0))
        put_tiles(mixed, row, laplace_step(centre, up, down))
        inner = [jnp.broadcast_to(state[row, pl.ds(s, 1), :], (8, WIDTH)) for s in (0, 4, 3, 7)]
        edge_centre = pick(left[0], left[1], right[0], right[1])
        outer = pick(left[2], left[3], right[2], right[3])
        put_tiles(edge, row, laplace_step(edge_centre, outer, pick(*inner)))
        return carry
    for var in range(4):
        wait_rows(from_prev, halo_recv.at[var], 32)
        wait_rows(from_next, halo_recv.at[4 + var], 32)
        lax.fori_loop(var * 8, var * 8 + 8, first, 0, unroll=8)
    mix_columns((mixed, stab), (edge, stab_edge))
    next(rounds)

    def second(row, carry):
        centre = get_tiles(mixed, row)
        sides = get_tiles(edge, row)
        side = [jnp.broadcast_to(sides[q:q + 1, :], (8, WIDTH)) for q in range(4)]
        up = jnp.where(x_of == 0, jnp.where(sub < 4, side[0], side[1]), pltpu.roll(centre, 1, 0))
        down = jnp.where(x_of == 3, jnp.where(sub < 4, side[2], side[3]), pltpu.roll(centre, 7, 0))
        put_tiles(mixed, row, laplace_step(centre, up, down))
        return carry
    lax.fori_loop(0, ROWS, second, 0, unroll=8)
    mix_columns((mixed, stab))
    wait_rows(to_next, halo_send.at[0], 128)
    wait_rows(to_prev, halo_send.at[1], 128)


def mark_sites(site, sites_at):
    columns = site[...] % 2048

    def body(n, carry):
        rows = pl.ds(pl.multiple_of(n * 256, 256), 256)
        place = lax.broadcasted_iota(jnp.int32, (256, LANES), 0) + n * 256
        for b in range(8):
            sites_at[rows, pl.ds(b * LANES, LANES)] = (place == columns[b:b + 1, :]).astype(F32).astype(BF16)
        return carry
    lax.fori_loop(0, 8, body, 0)


def mark_patch(index, weight, turned, chosen):
    turned[...] = jnp.transpose(jnp.concatenate([index[...].astype(F32), weight[...], jnp.zeros((96, LANES), F32)], axis=0))
    places = lax.broadcasted_iota(jnp.int32, (PATCH, OBS), 1)

    def body(n, carry):
        here = pltpu.roll(turned[...], LANES - n * 2, 1)
        for i in range(2):
            rows = pl.ds(pl.multiple_of((n * 2 + i) * PATCH, PATCH), PATCH)
            chosen[rows, :] = (places == here[:, i:i + 1].astype(jnp.int32)).astype(F32).astype(BF16)
        return carry
    lax.fori_loop(0, COLS // 2, body, 0)


def observe(mixed, site, sites_at, parts, obs):
    def body(n, carry):
        x, lt = div(n, 4), rem(n, 4)
        left = jnp.concatenate([mixed[pl.ds(lt * 256 + var * 64 + m * 4 + x, 8, stride=8), :] for m in range(2) for var in range(4)], axis=0)
        for part in range(3):
            piece = left.astype(BF16)
            parts[pl.ds(part * 64, 64), pl.ds(pl.multiple_of(n * LANES, LANES), LANES)] = piece
            left = left - piece.astype(F32)
        return carry
    lax.fori_loop(0, 16, body, 0, unroll=4)
    row = lax.broadcasted_iota(jnp.int32, (ROWS, LANES), 0)
    wanted = site[...] // 2048
    for b in range(0, 8, 2):
        found = dot(parts[...], sites_at[:, b * LANES:(b + 2) * LANES])
        found = found[:64] + (found[64:128] + found[128:])
        for i in range(2):
            for m in range(2):
                one = jnp.where(row == wanted[b + i:b + i + 1, :], found[m * ROWS:(m + 1) * ROWS, i * LANES:(i + 1) * LANES], 0.0)
                obs[pl.ds(m * 8 + b + i, 1), :] = jnp.sum(one, axis=0, keepdims=True)


def cut_columns(mixed, tiles):
    def body(n, carry):
        x, lt = div(n, 4), rem(n, 4)
        blocks = [mixed[pl.ds(lt * 256 + var * 64 + m * 4 + x, 8, stride=8), :] for m in range(2) for var in range(4)]
        for g, block in enumerate(block_transpose(blocks)):
            tiles[pl.ds(pl.multiple_of((x * 32 + lt * 8 + g) * 8, 8), 8), :] = block
        return carry
    lax.fori_loop(0, 16, body, 0, unroll=4)


def gather_obs(table, send_sems, plane_sems, x_sems, core_sem, me, tile):
    core, y, z, x = rem(me, 2), rem(div(me, 2), 8), rem(div(me, 16), 2), div(me, 32)

    def part(first, count):
        return table.at[pl.ds(pl.multiple_of(first * 16, count * 16), count * 16)]

    def slot(y_of, z_of):
        return part(core * 64 + x * 16 + y_of * 2 + z_of, 1)

    def pass_slot(one):
        for j in (2, 1, 3):
            send(one, one, send_sems.at[1], x_sems.at[j - 1], device_at(core, rem(x + j, 4), y, z), tile)
        send(one, one, send_sems.at[2], core_sem, device_at(1 - core, x, y, z), tile)
    own = slot(y, z)
    for i in (4, 3, 5, 2, 6, 1, 7, 0):
        send(own, own, send_sems.at[0], plane_sems.at[7 + i], device_at(core, x, rem(y + i, 8), 1 - z), tile)
        if i:
            send(own, own, send_sems.at[0], plane_sems.at[i - 1], device_at(core, x, rem(y + i, 8), z), tile)
    pass_slot(own)
    yield
    for i in (1, 7, 2, 6, 3, 5, 4):
        wait_rows(table, plane_sems.at[i - 1], 16)
        pass_slot(slot(rem(y + 8 - i, 8), z))
    for i in (0, 1, 7, 2, 6, 3, 5, 4):
        wait_rows(table, plane_sems.at[7 + i], 16)
        pass_slot(slot(rem(y + 8 - i, 8), 1 - z))
    yield
    for j in (1, 3, 2):
        wait_rows(table, x_sems.at[j - 1], 256)
        plane = part(core * 64 + rem(x + 4 - j, 4) * 16, 16)
        send(plane, plane, send_sems.at[2], core_sem, device_at(1 - core, x, y, z), tile)
    yield
    wait_rows(table, core_sem, 1024)
    yield
    wait_rows(table, send_sems.at[0], 16 * 15)
    wait_rows(table, send_sems.at[1], 256 * 3)
    wait_rows(table, send_sems.at[2], 1024)


def each_device(me, do, far=True, close=True):
    core, y, z, x = rem(me, 2), rem(div(me, 2), 8), rem(div(me, 16), 2), div(me, 32)

    def all_at(y_to, z_to, own):
        for i in (2, 1, 3, 0):
            for c in (1, 0):
                if not (own and i == 0 and c == 0):
                    do(device_at(rem(core + c, 2), rem(x + i, 4), y_to, z_to))

    def body(z_to):
        def one(n, carry):
            half = div(n + 1, 2)
            step = rem(12 + (2 * rem(n, 2) - 1) * half, 8)
            all_at(rem(y + step, 8), z_to, False)
            return carry
        return one
    if far:
        lax.fori_loop(0, 8, body(1 - z), 0)
    if close:
        lax.fori_loop(0, 7, body(z), 0)
        all_at(y, z, True)


def near(me):
    core, y, z, x = rem(me, 2), rem(div(me, 2), 8), rem(div(me, 16), 2), div(me, 32)
    return (
        [device_at(core, x, rem(y + i, 8), z) for i in range(1, 8)] + [device_at(core, x, rem(y + i, 8), 1 - z) for i in range(8)],
        [device_at(core, rem(x + i, 4), y, z) for i in range(1, 4)],
        [device_at(1 - core, x, y, z)],
    )


def greet(me, tile):
    barrier = pltpu.get_barrier_semaphore()
    for step in (1, 3):
        pl.semaphore_signal(barrier, inc=1, device_id=(me, rem(tile + step, 4)), device_id_type=MESH)
    for group in near(me):
        for to in group:
            pl.semaphore_signal(barrier, inc=1, device_id=(to, tile), device_id_type=MESH)
    yield
    pl.semaphore_wait(barrier, 2 + 15 + 3 + 1)


def pass_on(arrived, me, tile):
    for n, group in enumerate(near(me)):
        for to in group:
            pl.semaphore_signal(arrived.at[n], inc=1, device_id=(to, tile), device_id_type=MESH)
        yield
        pl.semaphore_wait(arrived.at[n], len(group))


def split(a):
    high = a.astype(BF16)
    return high, (a - high.astype(F32)).astype(BF16)


def dot(a, b):
    return jnp.dot(a, b, preferred_element_type=F32)


def dot_t(a, b):
    return lax.dot_general(a, b, (((1,), (1,)), ((), ())), preferred_element_type=F32)


def dot3(a, pair):
    high, low = split(a)
    return dot(high, pair[0]) + (dot(low, pair[0]) + dot(high, pair[1]))


def prepare(table, value, index, lookup, gap):
    total = table[pl.ds(0, 16), :]
    total = lax.fori_loop(1, MEM, lambda s, t: t + table[pl.ds(pl.multiple_of(s * 16, 16), 16), :], total)
    mean = (total[:8] + total[8:]) * (1.0 / MEMBERS)
    diff = value[...] - mean
    for b in range(8):
        for m in range(2):
            block = table[pl.ds(m * 8 + b, MEM, stride=16), :] - mean[b:b + 1, :]
            high, low = split(jnp.transpose(block))
            lookup[pl.ds(b * 128, 128), pl.ds(m * 128, 128)] = high
            lookup[pl.ds(b * 128, 128), pl.ds(256 + m * 128, 128)] = low
    indices = index[...]
    for part in range(2):
        own = indices[part * 8:part * 8 + 8]
        found = jnp.zeros((8, LANES), F32)
        for b in range(8):
            row = jnp.broadcast_to(diff[b:b + 1, :], (8, LANES))
            taken = jnp.take_along_axis(row, own % 128, axis=1, mode="promise_in_bounds")
            found = jnp.where(own // 128 == b, taken, found)
        gap[pl.ds(part * 8, 8), :] = found


def eye():
    shape = (PATCH, PATCH)
    return (lax.broadcasted_iota(jnp.int32, shape, 0) == lax.broadcasted_iota(jnp.int32, shape, 1)).astype(F32)


def stacked(a):
    return jnp.concatenate(split(a), axis=0)


def beside(a):
    return jnp.concatenate(split(a), axis=1)


def folded(p, rows, width):
    return (p[:rows, :width] + p[rows:, :width]) + (p[:rows, width:] + p[rows:, width:])


def pick_obs(chosen, lookup, picked):
    for n in range(2):
        rows = pl.ds(n * 1024, 1024)
        picked[rows, :] = dot(chosen[rows, :], lookup[...]).astype(BF16)


def patch_of(picked, c):
    return picked[pl.ds(pl.multiple_of(c * PATCH, PATCH), PATCH), :]


def sweep(turned, weight, gap, picked, turns, norms, shares, nudges):
    columns = range(COLS)
    one = eye()

    def c_rate(t):
        return 2.25 - 1.5 * t + 0.25 * t * t

    def h(t, y, square):
        return c_rate(t) * one + (0.25 * t - 1.5) * y + 0.25 * square

    def times(a, wide):
        return [folded(dot(stacked(m), k), m.shape[0], PATCH) for m, k in zip(a, wide)]
    patch = [patch_of(picked, c) for c in columns]
    both = [jnp.concatenate([p[:, :MEMBERS], p[:, MEMBERS:]], axis=0) for p in patch]
    cov = [folded(dot_t(q, q), PATCH, PATCH) for q in both]
    cov_w = [v * (weight[pl.ds(c, 1), :] * (1.0 / (MEMBERS - 1.0))) for v, c in zip(cov, columns)]
    t = []
    for c in columns:
        column = turned[:, COLS + c:COLS + c + 1] * (1.0 / (MEMBERS - 1.0))
        total = jnp.sum(cov_w[c] * (2.0 * one + cov[c] * column), axis=0, keepdims=True)
        total = jnp.sum(total, axis=1, keepdims=True)
        t.append(jnp.broadcast_to(1.0 / jnp.sqrt(MEMBERS + total), (1, PATCH)))
    k = [(one + v) * r for v, r in zip(cov_w, t)]
    k_wide = [beside(m) for m in k]
    k_square = times(k, k_wide)
    h_k = [h(r, m, q) for r, m, q in zip(t, k, k_square)]
    turn = times([2.25 * one - 1.5 * m + 0.25 * q for m, q in zip(k, k_square)], k_wide)
    t1 = [r * c_rate(r) for r in t]
    turn_wide = [beside(m) for m in turn]
    turn_square = times(turn, turn_wide)
    second = times([2.25 * one - 1.5 * m + 0.25 * q for m, q in zip(turn, turn_square)], turn_wide)
    f0, f1 = [1.5 - 0.5 * r for r in t], [1.5 - 0.5 * r for r in t1]
    f2 = [1.5 - 0.5 * r * c_rate(r) for r in t1]
    left = [jnp.concatenate([stacked(1.5 * one - 0.5 * m + a * b), stacked(a * c * b)], axis=1) for m, a, c, b in zip(turn, f0, f1, h_k)]
    right = [jnp.concatenate([beside(1.5 * one - 0.5 * m), beside(h(r, y, q))], axis=0) for m, r, y, q in zip(second, t1, turn, turn_square)]
    wide = [beside(-0.5 * folded(dot(a, b), PATCH, PATCH)) for a, b in zip(left, right)]
    first_row = lax.broadcasted_iota(jnp.int32, (16, PATCH), 0) == 0
    force = [jnp.where(first_row, weight[pl.ds(c, 1), :] * gap[pl.ds(c, 1), :], 0.0) for c in columns]
    share = [a * b * c for a, b, c in zip(f0, f1, f2)]
    ahead = [m - r * a for m, r, a in zip(times(force, k_wide), t, force)]
    force = [a * b + m for a, b, m in zip(share, force, times(ahead, wide))]
    for c in columns:
        turns[pl.ds(c * PATCH, PATCH), :] = wide[c]
        norms[pl.ds(c, 1), :] = t[c]
        shares[pl.ds(c, 1), :] = share[c]
        scale = jnp.sqrt(t[c])
        nudges[pl.ds(c, 1), :] = folded(dot(stacked(force[c]), patch[c]), 16, MEMBERS)[:1] * jnp.concatenate([scale, scale], axis=1)


def apply(fields, weight, picked, turns, norms, shares, nudges, analysed):
    columns = range(COLS)
    x = []
    for c in columns:
        parts = [fields[pl.ds((m * 4 + var) * 16 + c, 8, stride=128), :] for m in range(2) for var in range(4)]
        x.append(jnp.concatenate([jnp.concatenate(parts[:4], axis=0), jnp.concatenate(parts[4:], axis=0)], axis=1))
    mean = [jnp.sum(a, axis=1, keepdims=True) * (1.0 / MEMBERS) for a in x]
    pert = [a - b for a, b in zip(x, mean)]
    patch = [patch_of(picked, c) for c in columns]
    cross = []
    for c in columns:
        p = jnp.concatenate([patch[c][:, :MEMBERS], patch[c][:, MEMBERS:]], axis=0)
        scale = weight[pl.ds(c, 1), :] * norms[pl.ds(c, 1), :] * (1.0 / (MEMBERS - 1.0))
        cross.append(folded(dot_t(stacked(pert[c]), p), ROWS, PATCH) * scale)
    u = [folded(dot(stacked(cross[c]), patch_of(turns, c)), ROWS, PATCH) for c in columns]
    spread = [folded(dot(stacked(u[c]), patch[c]), ROWS, MEMBERS) for c in columns]
    for c in columns:
        scale, share = jnp.sqrt(norms[pl.ds(c, 1), :]), shares[pl.ds(c, 1), :]
        scale, share = jnp.concatenate([scale, scale], axis=1), jnp.concatenate([share, share], axis=1)
        moved = (share * pert[c] + spread[c]) * scale
        out = moved + (mean[c] + jnp.sum(moved * nudges[pl.ds(c, 1), :], axis=1, keepdims=True) * (1.0 / (MEMBERS - 1.0)))
        for m in range(2):
            for var in range(4):
                analysed[pl.ds((m * 4 + var) * 16 + c, 8, stride=128), :] = out[var * 8:var * 8 + 8, m * 128:m * 128 + 128]


def turn_members(src, dst):
    for level in range(LEVELS):
        dst[pl.ds(level * 128, 128), :] = jnp.transpose(src[pl.ds(level, MEM, stride=8), :])


def turn_back(src, dst):
    for level in range(LEVELS):
        dst[pl.ds(level, MEM, stride=8), :] = jnp.transpose(src[pl.ds(level * 128, 128), :])


def kernel(state_in, branch_in, site_in, value_in, index_in, weight_in, result,
           state, branch, site, value, weight, stab, stab_edge, to_next, to_prev, from_prev, from_next, mixed, edge, tiles, columns, obs, table,
           index, fields, lookup, turned, gap, analysed, picked, shares, turns, norms, nudges, outgoing, landed, placed, sites_at, parts, chosen,
           halo_send, halo_recv, send_sems, plane_sems, x_sems, core_sem, out_sems, in_sems, back_sems, load_sems, store_sems, arrived):
    me, tile = lax.axis_index("mem"), lax.axis_index("tile")
    greeting = greet(me, tile)
    next(greeting)
    loads = [pltpu.make_async_copy(state_in.at[:, m], state.at[:, pl.ds(m * 4, 4)], load_sems.at[m]) for m in range(2)]
    loads += [pltpu.make_async_copy(a, b, load_sems.at[2 + n]) for n, (a, b) in enumerate(
        ((branch_in, branch), (site_in, site), (value_in, value), (weight_in, weight),
         (index_in.at[0, pl.ds(pl.multiple_of(me * COLS, COLS), COLS)], index)))]
    for load in loads:
        load.start()

    def state_here():
        loads[0].wait()
        loads[1].wait()

    def meanwhile():
        for load in loads[3:]:
            load.wait()
        mark_sites(site, sites_at)
        mark_patch(index, weight, turned, chosen)
    rounds = pass_on(arrived, me, tile)
    forecast_body(state, branch, stab, stab_edge, to_next, to_prev, from_prev, from_next, mixed, edge, halo_send, halo_recv, me, tile,
                  greeting, rounds, state_here, loads[2].wait, meanwhile)
    slot = slot_of(me)
    here = pl.ds(pl.multiple_of(slot * 8, 8), 8)

    def to_owner(to):
        send(tiles.at[pl.ds(pl.multiple_of(to * 8, 8), 8)], columns.at[here], out_sems.at[0], in_sems.at[0], to, tile)
    observe(mixed, site, sites_at, parts, obs)
    table[pl.ds(pl.multiple_of(slot * 16, 16), 16), :] = obs[...]
    gather = gather_obs(table, send_sems, plane_sems, x_sems, core_sem, me, tile)
    next(gather)
    cut_columns(mixed, tiles)
    for _ in rounds:
        pass
    next(gather)
    each_device(me, to_owner)
    columns[here, :] = tiles[pl.ds(pl.multiple_of(me * 8, 8), 8), :]
    next(gather)
    next(gather)
    prepare(table, value, index, lookup, gap)
    pick_obs(chosen, lookup, picked)
    sweep(turned, weight, gap, picked, turns, norms, shares, nudges)
    for _ in gather:
        pass
    wait_rows(tiles, out_sems.at[0], 8 * (MEM - 1))
    wait_rows(columns, in_sems.at[0], 8 * (MEM - 1))
    turn_members(columns, fields)
    apply(fields, weight, picked, turns, norms, shares, nudges, analysed)
    turn_back(analysed, outgoing)
    mine = pl.ds(pl.multiple_of(me * 8, 8), 8)

    def give_back(to):
        send(outgoing.at[pl.ds(pl.multiple_of(slot_of(to) * 8, 8), 8)], landed.at[mine], out_sems.at[1], back_sems.at[div(me, 8)], to, tile)
    each_device(me, give_back)
    pltpu.make_async_copy(outgoing.at[here], landed.at[mine], back_sems.at[div(me, 8)]).start()
    whole = placed.reshape(4, ROWS, 8, LANES)
    stores = []
    for i in range(1, 5):
        lt = rem(div(me, 8) + i, 4)
        for x in range(4):
            wait_rows(landed, back_sems.at[x * 4 + lt], 64)
        for x in range(4):
            place(landed, placed, x, lt)
        for m in range(2):
            lanes = pl.ds(pl.multiple_of(lt * LANES, LANES), LANES)
            stores.append(pltpu.make_async_copy(whole.at[lt, :, pl.ds(m * 4, 4)], result.at[:, m, :, lanes], store_sems.at[i * 2 - 2 + m]))
            stores[-1].start()
    wait_rows(outgoing, out_sems.at[1], 8 * (MEM - 1))
    for store in stores:
        store.wait()


def copy_kernel(source, result, held, sems):
    parts = [pl.ds(n * 8, 8) for n in range(4)]
    reads = [pltpu.make_async_copy(source.at[p], held.at[p], sems.at[n]) for n, p in enumerate(parts)]
    writes = [pltpu.make_async_copy(held.at[p], result.at[p], sems.at[4 + n]) for n, p in enumerate(parts)]
    for read in reads:
        read.start()
    for read, write in zip(reads, writes):
        read.wait()
        write.start()
    for write in writes:
        write.wait()


def place(landed, result, x, lt):
    blocks = [landed[pl.ds(pl.multiple_of((x * 32 + lt * 8 + g) * 8, 8), 8), :] for g in range(8)]
    blocks = block_transpose(blocks)
    for m in range(2):
        for var in range(4):
            result[pl.ds(lt * 256 + var * 64 + m * 4 + x, 8, stride=8), :] = blocks[m * 4 + var]


def shape(*dims, dtype=F32):
    return jax.ShapeDtypeStruct(dims, dtype)


def per_device(state, branch, obs_site, obs_value, patch_index, patch_weight):
    dma = pltpu.SemaphoreType.DMA
    regular = pltpu.SemaphoreType.REGULAR

    def rows(n, width=LANES, dtype=F32):
        return pltpu.VMEM((n, width), dtype)
    result = pl.pallas_call(
        kernel,
        name="forecast_analysis",
        out_shape=shape(ROWS, 2, 4, WIDTH),
        in_specs=[HBM] * 6,
        out_specs=HBM,
        scratch_shapes=[
            pltpu.VMEM((ROWS, 8, WIDTH), F32), pltpu.VMEM((16, WIDTH), jnp.int32), rows(8, dtype=jnp.int32), rows(8), rows(COLS),
            rows(64), rows(64), rows(128, WIDTH), rows(128, WIDTH), rows(128, WIDTH), rows(128, WIDTH),
            rows(1024), rows(1024), rows(1024), rows(1024), rows(16), rows(MEM * 16),
            rows(COLS, LANES, jnp.int32), rows(1024), rows(OBS, 2 * MEMBERS, BF16), rows(LANES), rows(COLS), rows(1024),
            rows(COLS * PATCH, 2 * MEMBERS, BF16), rows(COLS), rows(COLS * PATCH, 2 * PATCH, BF16),
            rows(COLS), rows(COLS, MEMBERS), rows(1024), rows(1024), rows(1024),
            rows(2048, OBS, BF16), rows(192, 2048, BF16), rows(COLS * PATCH, OBS, BF16),
            dma((2,)), dma((8,)), dma((3,)), dma((15,)), dma((3,)), dma(()), dma((2,)), dma((1,)), dma((16,)), dma((7,)), dma((8,)), regular((3,)),
        ],
        compiler_params=pltpu.CompilerParams(collective_id=1, has_side_effects=True, vmem_limit_bytes=60 * 1024 * 1024),
    )(state.reshape(ROWS, 2, 4, WIDTH), branch, obs_site.reshape(8, LANES), obs_value.reshape(8, LANES), patch_index, patch_weight.reshape(COLS, LANES))
    result = pl.pallas_call(
        copy_kernel,
        name="copy_out",
        out_shape=shape(ROWS, 2, 4, WIDTH),
        in_specs=[HBM],
        out_specs=HBM,
        scratch_shapes=[pltpu.VMEM((ROWS, 2, 4, WIDTH), F32), dma((8,))],
        compiler_params=pltpu.CompilerParams(vmem_limit_bytes=60 * 1024 * 1024),
    )(result)
    return result.reshape(state.shape)


def solution(mesh):
    placed = (
        P(None, None, "mem", "tile", None),
        P(),
        P("tile", None),
        P("tile", None),
        P("tile", None, None),
        P("tile", "mem", None),
    )
    return jax.shard_map(
        per_device,
        mesh=mesh,
        in_specs=placed,
        out_specs=P(None, None, "mem", "tile", None),
        check_vma=False,
    )
```
